256 devices in a mesh: orb: 4 (over z_hi), gx: 16 (over x, y), gy: 4 (over z_lo, core).
Axes of the slice: x: 4, y: 4, z: 8 (z_hi: 4, z_lo: 2; z = z_hi * 2 + z_lo), core: 2. Of those that a mesh axis runs over, the one named last changes fastest.
Arguments:
- orbitals: float32 [32, 160, 160, 128], P('orb', 'gx', 'gy'), may hold values from -1.6 to 1.6
- dielectric: float32 [160, 160, 128], P('gx', 'gy'), may hold values from 0.25 to 2
- owner_group: int32 [2], replicated, may hold values from 0 to 3, as said below
- block_slots: int32 [2, 4], replicated, may hold values from 0 to 7, as said below
Outputs:
- exchange: float32 [2, 4, 160, 160, 128], P(None, 'orb', 'gx', 'gy')
The draws below stay inside these ranges and needn't reach their ends.
Inputs may be any that keep to these rules, and one draw needn't show every extreme that they name: `block_slots`: over all windows together, every slot 0 to 7 appears exactly once. `owner_group`: different windows have different owners.
All inputs are finite; a program needn't handle non-finite values.
Results may differ from the reference program's by a relative error of at most 0.00002.
Values sent between devices are 32-bit elements; how exact they have to be, the bound alone decides.
A program may use at most 192 MiB of HBM per device.

```python
import math
import jax
import jax.numpy as jnp
from jax import lax

RES = 8
BLOCK = 4
NZ = 128
WINDOWS = 2
NORB = 32
NX = 160
NY = 160
N_ORB = 4


def draw_orbitals(key, part):
    key = jax.random.fold_in(key, 5)
    extent = (NORB, NX, NY, NZ)
    return jnp.clip(0.4 * jax.random.normal(key, extent, jnp.float32), -1.6, 1.6)


def draw_owner_group(key, part):
    key = jax.random.fold_in(key, 7)
    first_key, second_key = jax.random.split(key)
    others = jax.random.permutation(second_key, N_ORB - 1)[:WINDOWS].astype(jnp.int32)
    placed = jax.random.randint(first_key, (), 0, WINDOWS).astype(jnp.int32)
    window_ids = jnp.arange(WINDOWS, dtype=jnp.int32)
    return jnp.where(window_ids == placed, jnp.int32(N_ORB - 1), others).astype(jnp.int32)


def draw_block_slots(key, part):
    key = jax.random.fold_in(key, 11)
    shuffled = jax.random.permutation(key, RES)
    return shuffled.reshape(WINDOWS, BLOCK).astype(jnp.int32)


def shard_levels(key, shape, shards, least, largest):
    level = 1.0
    for dim, blocks in shards:
        draws = jax.random.uniform(jax.random.fold_in(jax.random.fold_in(key, 6), dim), (blocks,), jnp.float32, least / len(shards), largest / len(shards))
        level = level * jnp.repeat(jnp.exp(draws), shape[dim] // blocks).reshape((-1,) + (1,) * (len(shape) - 1 - dim))
    return level


def setup_inputs(seed: int = 0) -> dict:
    splits = jax.random.split(jax.random.key(seed), 5)
    orbitals = draw_orbitals(jax.random.fold_in(splits[4], 71), 0)
    dielectric = jnp.clip(jnp.exp(math.log(2.0) - 2.0794415 * jax.random.uniform(splits[1], (NX, NY, NZ), jnp.float32) ** shard_levels(splits[1], (NX, NY, NZ), ((0, 16), (1, 4)), -0.2, 0.2)), 0.25, 2.0)
    owner_group = draw_owner_group(jax.random.fold_in(splits[4], 71), 0)
    block_slots = draw_block_slots(jax.random.fold_in(splits[4], 71), 0)
    return {"orbitals": orbitals, "dielectric": dielectric, "owner_group": owner_group, "block_slots": block_slots}


FOUR_PI = 4.0 * math.pi
MIXING = 0.25
LOWEST = 0.5
HIGHEST = 24.0
SPECTRUM_MID = (HIGHEST + LOWEST) / 2.0
SPECTRUM_HALF = (HIGHEST - LOWEST) / 2.0
SPECTRUM_RATIO = SPECTRUM_MID / SPECTRUM_HALF
RATE_ZERO = 1.0 / SPECTRUM_RATIO
RATE_ONE = 1.0 / (2.0 * SPECTRUM_RATIO - RATE_ZERO)
RATE_TWO = 1.0 / (2.0 * SPECTRUM_RATIO - RATE_ONE)
KEEP_FACTORS = (RATE_ONE * RATE_ZERO, RATE_TWO * RATE_ONE)
STEP_FACTORS = (2.0 * RATE_ONE / SPECTRUM_HALF, 2.0 * RATE_TWO / SPECTRUM_HALF)


def operate(padded, coef_wide):
    center = padded[:, 1:-1, 1:-1, :]
    coef_mid = coef_wide[1:-1, 1:-1, :]
    neighbours = [
        (padded[:, 2:, 1:-1, :], coef_wide[2:, 1:-1, :]),
        (padded[:, :-2, 1:-1, :], coef_wide[:-2, 1:-1, :]),
        (padded[:, 1:-1, 2:, :], coef_wide[1:-1, 2:, :]),
        (padded[:, 1:-1, :-2, :], coef_wide[1:-1, :-2, :]),
    ]
    summed = jnp.zeros_like(center)
    for neighbour, coef_near in neighbours:
        summed = summed + 0.5 * (coef_mid + coef_near) * (center - neighbour)
    depth_pad = jnp.pad(center, ((0, 0), (0, 0), (0, 0), (1, 1)))
    coef_depth = jnp.pad(coef_mid, ((0, 0), (0, 0), (1, 1)), mode="edge")
    summed = summed + 0.5 * (coef_mid + coef_depth[:, :, 2:]) * (center - depth_pad[:, :, :, 2:])
    summed = summed + 0.5 * (coef_mid + coef_depth[:, :, :-2]) * (center - depth_pad[:, :, :, :-2])
    return summed


def chebyshev(source, coef_wide):
    iterate = source / SPECTRUM_MID
    search = iterate
    for section in range(2):
        widened = jnp.pad(iterate, ((0, 0), (1, 1), (1, 1), (0, 0)), mode="wrap")
        misfit = source - operate(widened, coef_wide)
        search = KEEP_FACTORS[section] * search + STEP_FACTORS[section] * misfit
        iterate = iterate + search
    return iterate


def reference(orbitals, dielectric, owner_group, block_slots):
    coef_wide = jnp.pad(dielectric, ((1, 1), (1, 1), (0, 0)), mode="wrap")
    results = []
    for window in range(WINDOWS):
        chosen = (owner_group[window] * RES + block_slots[window]).astype(jnp.int32)
        block_fields = jnp.take(orbitals, chosen, axis=0)
        scaled = FOUR_PI * block_fields

        def accumulate(running, orbital):
            potential = chebyshev(scaled * orbital[None], coef_wide)
            return running + potential * orbital[None], None

        running, unused = lax.scan(accumulate, jnp.zeros(block_fields.shape, jnp.float32), orbitals)
        results.append(-MIXING * running)
    return jnp.stack(results)
```

```python
import math

import jax
import jax.numpy as jnp
from jax import lax
from jax.experimental import pallas as pl
from jax.experimental.pallas import tpu as pltpu
from jax.sharding import PartitionSpec as P

MESH = pl.DeviceIdType.MESH
F32 = jnp.float32

MIXING = 0.25
LOWEST = 0.5
HIGHEST = 24.0
MID = (HIGHEST + LOWEST) / 2.0
HALF = (HIGHEST - LOWEST) / 2.0
RATIO = MID / HALF
R0 = 1.0 / RATIO
R1 = 1.0 / (2.0 * RATIO - R0)
R2 = 1.0 / (2.0 * RATIO - R1)
K1, K2 = R1 * R0, R2 * R1
S1, S2 = 2.0 * R1 / HALF, 2.0 * R2 / HALF
Q = 1.0 / MID
ALPHA, BETA = K1 * Q + S1, S1 * Q
SCALE = -MIXING * 4.0 * math.pi
C0 = SCALE * (Q + ALPHA + K2 * ALPHA + S2)
C1 = -SCALE * (BETA + K2 * BETA + S2 * (Q + ALPHA))
C2 = SCALE * S2 * BETA

GROUPS = 4
RES = 8
ORBS = 32
XS = 10
SUB = 10
ROW = 14
PAIRS = 5
BASE = 18
FIRST = BASE + 2 * ROW + 2
LEAD = 32
ROWS = 240
CHUNKS = 17
LEAD_CHUNKS = 4
COUP = (CHUNKS + LEAD_CHUNKS) * 8
STARTS = (-2, 10, 18, 30)
ORDER = (0, 4, 1, 2, 3)


def kernel(
    orb, diel, owner, slots, out,
    send, rb, sib_s, sib_r, ys, yr, ds_, db, w, wd, kx, ky, kz, dd, coup, dens, flat, ob, orr,
    s_send, r_send, l_send, s_sib, r_sib, s_y, r_y, s_x, r_x, s_xs, r_xs, s_d, r_d, l_d, s_dx, r_dx, s_o, r_o, l_o,
):
    g, gx, gy = lax.axis_index("orb"), lax.axis_index("gx"), lax.axis_index("gy")
    zl, c = gy // 2, lax.rem(gy, 2)
    home = g // 2
    mine = c == home
    part = lax.rem(g, 2)
    sibling = (g, gx, 2 * zl + 1 - c)
    left, right = (g, lax.rem(gx + 15, 16), gy), (g, lax.rem(gx + 1, 16), gy)
    down, up = (g, gx, lax.rem(gy + 3, 4)), (g, gx, lax.rem(gy + 1, 4))

    def remote(src, dst, ss, rs, to):
        return pltpu.make_async_remote_copy(
            src_ref=src, dst_ref=dst, send_sem=ss, recv_sem=rs, device_id=to, device_id_type=MESH
        )

    barrier = pltpu.get_barrier_semaphore()
    for dg in range(GROUPS):
        for dc in range(2):
            if dg or dc:
                to = (lax.rem(g + dg, GROUPS), gx, 2 * zl + (c if dc == 0 else 1 - c))
                pl.semaphore_signal(barrier, inc=1, device_id=to, device_id_type=MESH)
    across = (g, gx, lax.rem(gy + 3 + 2 * c, 4))
    for to in (left, right, across):
        pl.semaphore_signal(barrier, inc=1, device_id=to, device_id_type=MESH)
    pl.semaphore_wait(barrier, 10)

    def pack_ends(f, carry):
        for x in range(XS):
            ys[0, f, 2 * x : 2 * x + 2, :] = orb[f, x, 0:2, :]
            ys[1, f, 2 * x : 2 * x + 2, :] = orb[f, x, 38:40, :]
        return carry

    lax.fori_loop(0, RES, pack_ends, 0)
    for x in range(XS):
        ys[0, RES, 2 * x : 2 * x + 2, :] = diel[x, 0:2, :]
        ys[1, RES, 2 * x : 2 * x + 2, :] = diel[x, 38:40, :]
    to_down = remote(ys.at[0], yr.at[1], s_y.at[0], r_y.at[1], down)
    to_up = remote(ys.at[1], yr.at[0], s_y.at[1], r_y.at[0], up)
    to_down.start()
    to_up.start()

    def pack(p, which):
        def body(f, carry):
            for xx in range(2):
                x = 2 * p + xx
                at = pl.multiple_of(24 * f, 8)
                for wi in which:
                    o = 12 * xx
                    if wi == 0:
                        send[p, wi, f, o : o + 2, :] = yr[0, f, 2 * x : 2 * x + 2, :]
                        send[p, wi, f, o + 2 : o + 12, :] = orb[f, x, 0:10, :]
                    elif wi == 3:
                        send[p, wi, f, o : o + 10, :] = orb[f, x, 30:40, :]
                        send[p, wi, f, o + 10 : o + 12, :] = yr[1, f, 2 * x : 2 * x + 2, :]
                    else:
                        send[p, wi, f, o : o + 12, :] = orb[f, x, STARTS[wi] : STARTS[wi] + 12, :]
            return carry

        lax.fori_loop(0, RES, body, 0)

    def share_copy(p, wi):
        to = (2 * c + wi // 2, gx, 2 * zl + wi % 2)
        here = jnp.logical_and(to[0] == g, c == wi % 2)
        away = remote(send.at[p, wi], rb.at[p + 1, g], s_send.at[p, wi], r_send.at[p, g], to)
        near = pltpu.make_async_copy(send.at[p, wi], rb.at[p + 1, g], l_send.at[p])
        return here, away, near

    def share_start(p, wi):
        here, away, near = share_copy(p, wi)
        pl.when(here)(near.start)
        pl.when(jnp.logical_not(here))(away.start)

    def share_sent(p, wi):
        here, away, near = share_copy(p, wi)
        pl.when(jnp.logical_not(here))(away.wait_send)

    def share_arrived(p, source):
        near_one = jnp.logical_and(g == source, mine)
        near = pltpu.make_async_copy(send.at[p, 0], rb.at[p + 1, source], l_send.at[p])
        away = remote(send.at[p, 0], rb.at[p + 1, source], s_send.at[p, 0], r_send.at[p, source], sibling)
        pl.when(near_one)(near.wait)
        pl.when(jnp.logical_not(near_one))(away.wait_recv)

    for p in ORDER[:2]:
        pack(p, (1, 2))
        share_start(p, 1)
        share_start(p, 2)
    to_down.wait()
    to_up.wait()
    for p in ORDER[:2]:
        pack(p, (0, 3))
        share_start(p, 0)
        share_start(p, 3)

    for ch in range(2):
        for ph in range(2):

            @pl.when(jnp.logical_and(mine, jnp.logical_and(c == ch, part == ph)))
            def _():
                for k in range(2):
                    wi = 2 * ph + k
                    for x in range(XS):
                        p, o = x // 2, ROW * (x % 2)
                        if wi == 0:
                            ds_[k, p, o : o + 2, :] = yr[0, RES, 2 * x : 2 * x + 2, :]
                            ds_[k, p, o + 2 : o + 14, :] = diel[x, 0:12, :]
                        elif wi == 3:
                            ds_[k, p, o : o + 12, :] = diel[x, 28:40, :]
                            ds_[k, p, o + 12 : o + 14, :] = yr[1, RES, 2 * x : 2 * x + 2, :]
                        else:
                            ds_[k, p, o : o + 14, :] = diel[x, 10 * wi - 2 : 10 * wi + 12, :]
                near = pltpu.make_async_copy(ds_.at[ch], db.at[pl.ds(1, PAIRS)], l_d)
                away = remote(ds_.at[1 - ch], db.at[pl.ds(1, PAIRS)], s_d, r_d, sibling)
                near.start()
                away.start()
                near.wait()
                away.wait_send()

    for p in ORDER[2:]:
        pack(p, (0, 1, 2, 3))
        for wi in range(4):
            share_start(p, wi)

    @pl.when(jnp.logical_not(mine))
    def _():
        remote(ds_.at[0], db.at[pl.ds(1, PAIRS)], s_d, r_d, sibling).wait_recv()

    d_left = remote(db.at[1], db.at[6], s_dx.at[0], r_dx.at[0], left)
    d_right = remote(db.at[5], db.at[0], s_dx.at[1], r_dx.at[1], right)
    d_left.start()
    d_right.start()
    d_left.wait()
    d_right.wait()
    wd[...] = jnp.zeros_like(wd)
    for s in range(7):
        wd[BASE + 28 * s : BASE + 28 * s + 28, :] = db[s, 0:28, :]

    lane = lax.broadcasted_iota(jnp.int32, (8, 128), 1)
    top, bottom = lane == 127, lane == 0

    def ahead(v, n=1):
        return pltpu.roll(v, 128 - n, 1)

    def at(ref, r, n=0):
        return ref[r + n : r + n + 8, :]

    for i in range(29):
        r = 8 * i
        if r + 14 + 8 > ROWS:
            break
        e, ex, ey = at(wd, r), at(wd, r, 14), at(wd, r, 1)
        kx[r : r + 8, :] = 0.5 * (e + ex)
        ky[r : r + 8, :] = 0.5 * (e + ey)
        kz[r : r + 8, :] = jnp.where(top, 0.0, 0.5 * (e + ahead(e)))

    def squared(r):
        e = at(wd, r)
        x1, x0, y1, y0 = at(kx, r), at(kx, r, -14), at(ky, r), at(ky, r, -1)
        z1 = at(kz, r)
        z0 = pltpu.roll(z1, 1, 1)
        ends = jnp.where(jnp.logical_or(top, bottom), e, 0.0)
        total = x1 + x0 + y1 + y0 + z1 + z0 + ends
        squares = x1 * x1 + x0 * x0 + y1 * y1 + y0 * y0 + z1 * z1 + z0 * z0
        return total, squares

    for i in range(2, 27):
        r = 8 * i
        total, squares = squared(r)
        dd[0, r : r + 8, :] = total
        dd[1, r : r + 8, :] = squares

    def couplings(k):
        r = FIRST + 8 * k
        d0, sq = at(dd.at[0], r), at(dd.at[1], r)
        x1, y1, z1 = at(kx, r), at(ky, r), at(kz, r)
        dx, dy = at(dd.at[0], r, 14), at(dd.at[0], r, 1)
        xx, yx, zx = at(kx, r, 14), at(ky, r, 14), at(kz, r, 14)
        xy, yy, zy = at(kx, r, 1), at(ky, r, 1), at(kz, r, 1)
        dz, xz, yz, zz = ahead(d0), ahead(x1), ahead(y1), ahead(z1)
        values = (
            C0 + C1 * d0 + C2 * (d0 * d0 + sq),
            -x1 * (C1 + C2 * (d0 + dx)),
            -y1 * (C1 + C2 * (d0 + dy)),
            -z1 * (C1 + C2 * (d0 + dz)),
            C2 * (x1 * xx),
            C2 * (y1 * yy),
            C2 * (z1 * zz),
            C2 * (x1 * yx + y1 * xy),
            C2 * (x1 * y1 + xy * yx),
            C2 * (x1 * zx + z1 * xz),
            C2 * (x1 * z1 + xz * zx),
            C2 * (y1 * zy + z1 * yz),
            C2 * (y1 * z1 + yz * zy),
        )
        for n, v in enumerate(values):
            coup[n, LEAD + 8 * k : LEAD + 8 * k + 8, :] = v

    for k in range(-LEAD_CHUNKS, CHUNKS):
        couplings(k)

    def sib_copy(p):
        return remote(sib_s.at[p], sib_r.at[p + 1], s_sib.at[p], r_sib.at[p], sibling)

    def arrive(p):
        for source in range(GROUPS):
            share_arrived(p, source)
        for ch in range(2):

            @pl.when(c == ch)
            def _():
                def body(o, carry):
                    q, f = o // RES, lax.rem(o, RES)
                    for xx in range(2):
                        a = 12 * xx + (10 if ch == 0 else 0)
                        sib_s[p, o, 2 * xx : 2 * xx + 2, :] = rb[p + 1, q, f, a : a + 2, :]
                    return carry

                lax.fori_loop(0, ORBS, body, 0)

        sib_copy(p).start()

    def edge_copies(p):
        to, slot, n = (left, 6, 0) if p == 0 else (right, 0, 1)
        return (
            remote(rb.at[p + 1], rb.at[slot], s_x.at[n], r_x.at[n], to),
            remote(sib_r.at[p + 1], sib_r.at[slot], s_xs.at[n], r_xs.at[n], to),
        )

    def unpack(slot):
        for ch in range(2):

            @pl.when(c == ch)
            def _():
                def body(o, carry):
                    q, f = o // RES, lax.rem(o, RES)
                    for xx in range(2):
                        r = BASE + 28 * slot + ROW * xx
                        m = r + (0 if ch == 0 else 2)
                        h = r + (12 if ch == 0 else 0)
                        w[o, m : m + 12, :] = rb[slot, q, f, 12 * xx : 12 * xx + 12, :]
                        w[o, h : h + 2, :] = sib_r[slot, o, 2 * xx : 2 * xx + 2, :]
                    return carry

                lax.fori_loop(0, ORBS, body, 0)

    for p in (0, 4):
        arrive(p)
        edge_copies(p)[0].start()
    for p in (0, 4):
        sib_copy(p).wait()
        edge_copies(p)[1].start()
        unpack(p + 1)
    for p in (1, 2, 3):
        arrive(p)
        sib_copy(p).wait()
        unpack(p + 1)
    for p in (0, 4):
        for e in edge_copies(p):
            e.wait()
    unpack(0)
    unpack(6)

    def density(k):
        r = FIRST + 8 * k

        def body(o, acc):
            a, b, b2 = at(w.at[o], r), at(w.at[o], r, 14), at(w.at[o], r, 28)
            y1, y2, xy = at(w.at[o], r, 1), at(w.at[o], r, 2), at(w.at[o], r, 15)
            az, az2, bz, yz = ahead(a), ahead(a, 2), ahead(b), ahead(y1)
            terms = (
                a * a, a * b, a * y1, a * az, a * b2, a * y2, a * az2,
                a * xy, b * y1, a * bz, az * b, a * yz, az * y1,
            )
            return tuple(s + t for s, t in zip(acc, terms))

        acc = lax.fori_loop(0, ORBS, body, (jnp.zeros((8, 128), F32),) * 13, unroll=4)
        for n in range(13):
            s = slice(LEAD + 8 * k, LEAD + 8 * k + 8)
            dens[n, s, :] = coup[n, s, :] * acc[n]

    def apply(k):
        r = FIRST + 8 * k
        d = LEAD + 8 * k

        def m(n, back=0):
            return dens[n, d - back : d - back + 8, :]

        def behind(v, n=1):
            return pltpu.roll(v, n, 1)

        flat_terms = (
            (0, m(0)), (14, m(1)), (-14, m(1, 14)), (1, m(2)), (-1, m(2, 1)), (28, m(4)), (-28, m(4, 28)),
            (2, m(5)), (-2, m(5, 2)), (15, m(7)), (-15, m(7, 15)), (13, m(8, 1)), (-13, m(8, 14)),
        )
        lower = ((0, m(3)), (14, m(10)), (-14, m(9, 14)), (1, m(12)), (-1, m(11, 1)))
        upper = (
            (0, behind(m(3))), (14, behind(m(9))), (-14, behind(m(10, 14))), (1, behind(m(11))), (-1, behind(m(12, 1))),
        )
        lower2, upper2 = m(6), behind(m(6), 2)

        def body(n, carry):
            window, b = n // 4, lax.rem(n, 4)
            o = owner[window] * RES + slots[window, b]
            v = {s: w[o, r + s : r + s + 8, :] for s, _ in flat_terms}

            def dot(terms):
                total = None
                for s, coefficient in terms:
                    t = coefficient * v[s]
                    total = t if total is None else total + t
                return total

            res = dot(flat_terms) + behind(dot(lower)) + ahead(dot(upper))
            res = res + behind(lower2 * v[0], 2) + ahead(upper2 * v[0], 2)
            flat[n, 8 * k : 8 * k + 8, :] = res
            return carry

        lax.fori_loop(0, 8, body, 0)

    for k in range(-LEAD_CHUNKS, CHUNKS):
        density(k)
    for k in range(CHUNKS):
        apply(k)

    def pack_out(j, carry):
        for window in range(2):
            for x in range(XS):
                o = 100 * window + 10 * x
                ob[j, o : o + 10, :] = flat[4 * window + j, ROW * x : ROW * x + 10, :]
        return carry

    lax.fori_loop(0, GROUPS, pack_out, 0)

    def out_copy(j):
        to = (j, gx, 2 * zl + home)
        here = jnp.logical_and(g == j, mine)
        slot = 2 * part + c
        away = remote(ob.at[j], orr.at[slot], s_o.at[j], r_o.at[slot], to)
        near = pltpu.make_async_copy(ob.at[j], orr.at[slot], l_o)
        return here, away, near

    for j in range(GROUPS):
        here, away, near = out_copy(j)
        pl.when(here)(near.start)
        pl.when(jnp.logical_not(here))(away.start)
    for wi in range(4):
        here = jnp.logical_and(2 * c + wi // 2 == g, c == wi % 2)
        away = remote(ob.at[0], orr.at[wi], s_o.at[0], r_o.at[wi], sibling)
        near = pltpu.make_async_copy(ob.at[0], orr.at[wi], l_o)
        pl.when(here)(near.wait)
        pl.when(jnp.logical_not(here))(away.wait_recv)
        for window in range(2):
            for x in range(XS):
                o = 100 * window + 10 * x
                out[window, 0, x, 10 * wi : 10 * wi + 10, :] = orr[wi, o : o + 10, :]

    for p in range(PAIRS):
        for wi in range(4):
            share_sent(p, wi)
    for j in range(GROUPS):
        here, away, near = out_copy(j)
        pl.when(jnp.logical_not(here))(away.wait_send)


def shards(orbitals, dielectric, owner_group, block_slots):
    dma = pltpu.SemaphoreType.DMA
    vmem = pl.BlockSpec(memory_space=pltpu.VMEM)
    smem = pl.BlockSpec(memory_space=pltpu.SMEM)

    def buf(*shape):
        return pltpu.VMEM(shape + (128,), F32)

    return pl.pallas_call(
        kernel,
        out_shape=jax.ShapeDtypeStruct((2, 1, 10, 40, 128), F32),
        in_specs=[vmem, vmem, smem, smem],
        out_specs=vmem,
        scratch_shapes=[
            buf(PAIRS, 4, RES, 24), buf(7, GROUPS, RES, 24), buf(PAIRS, ORBS, 8), buf(7, ORBS, 8),
            buf(2, RES + 1, 24), buf(2, RES + 1, 24), buf(2, PAIRS, 32), buf(7, 32),
            buf(ORBS, ROWS), buf(ROWS), buf(ROWS), buf(ROWS), buf(ROWS), buf(2, ROWS),
            buf(13, COUP), buf(13, COUP), buf(8, CHUNKS * 8), buf(GROUPS, 200), buf(4, 200),
            dma((PAIRS, 4)), dma((PAIRS, 4)), dma((PAIRS,)),
            dma((PAIRS,)), dma((PAIRS,)), dma((2,)), dma((2,)), dma((2,)), dma((2,)), dma((2,)), dma((2,)),
            dma, dma, dma, dma((2,)), dma((2,)), dma((GROUPS,)), dma((4,)), dma,
        ],
        compiler_params=pltpu.CompilerParams(collective_id=0, has_side_effects=True, vmem_limit_bytes=40 << 20),
        cost_estimate=pl.CostEstimate(flops=60_000_000, bytes_accessed=2_500_000, transcendentals=0),
    )(orbitals, dielectric, owner_group, block_slots)


def solution(mesh):
    in_specs = (P("orb", "gx", "gy", None), P("gx", "gy", None), P(), P())
    out_specs = P(None, "orb", "gx", "gy", None)
    return jax.shard_map(shards, mesh=mesh, in_specs=in_specs, out_specs=out_specs, check_vma=False)
```

```python
import math

import jax
import jax.numpy as jnp
from jax import lax
from jax.experimental import pallas as pl
from jax.experimental.pallas import tpu as pltpu
from jax.sharding import PartitionSpec as P

MESH = pl.DeviceIdType.MESH
F32 = jnp.float32

MIXING = 0.25
LOWEST = 0.5
HIGHEST = 24.0
MID = (HIGHEST + LOWEST) / 2.0
HALF = (HIGHEST - LOWEST) / 2.0
RATIO = MID / HALF
R0 = 1.0 / RATIO
R1 = 1.0 / (2.0 * RATIO - R0)
R2 = 1.0 / (2.0 * RATIO - R1)
K1, K2 = R1 * R0, R2 * R1
S1, S2 = 2.0 * R1 / HALF, 2.0 * R2 / HALF
Q = 1.0 / MID
ALPHA, BETA = K1 * Q + S1, S1 * Q
SCALE = -MIXING * 4.0 * math.pi
C0 = SCALE * (Q + ALPHA + K2 * ALPHA + S2)
C1 = -SCALE * (BETA + K2 * BETA + S2 * (Q + ALPHA))
C2 = SCALE * S2 * BETA

GROUPS = 4
RES = 8
ORBS = 32
XS = 10
SUB = 10
ROW = 14
PAIRS = 5
BASE = 18
FIRST = BASE + 2 * ROW + 2
LEAD = 32
ROWS = 240
CHUNKS = 17
LEAD_CHUNKS = 4
COUP = (CHUNKS + LEAD_CHUNKS) * 8
STARTS = (-2, 10, 18, 30)
ORDER = (0, 4, 1, 3, 2)
PIECES = ((0, 2), (8, 2), (2, 6))


def kernel(
    orb_in, diel_in, owner_in, slots_in, out,
    orb, diel, owner, slots, s_in, s_small, send, rb, sib_s, sib_r, ys, yr, ds_, db, w, wz, wz2, wd, kx, ky, kz, dd, coup, dens, flat, ob0, ob1, ob2, or0, or1, or2,
    s_send, r_send, l_send, s_sib, r_sib, s_y, r_y, s_x, r_x, s_xs, r_xs, s_d, r_d, l_d, s_dx, r_dx, s_o, r_o, l_o,
):
    g, gx, gy = lax.axis_index("orb"), lax.axis_index("gx"), lax.axis_index("gy")
    zl, c = gy // 2, lax.rem(gy, 2)
    home = g // 2
    mine = c == home
    part = lax.rem(g, 2)
    sibling = (g, gx, 2 * zl + 1 - c)
    left, right = (g, lax.rem(gx + 15, 16), gy), (g, lax.rem(gx + 1, 16), gy)
    down, up = (g, gx, lax.rem(gy + 3, 4)), (g, gx, lax.rem(gy + 1, 4))

    def remote(src, dst, ss, rs, to):
        return pltpu.make_async_remote_copy(
            src_ref=src, dst_ref=dst, send_sem=ss, recv_sem=rs, device_id=to, device_id_type=MESH
        )

    loads = [
        pltpu.make_async_copy(orb_in.at[:, pl.ds(2 * p, 2)], orb.at[:, pl.ds(2 * p, 2)], s_in.at[p]) for p in range(PAIRS)
    ]
    small = [
        pltpu.make_async_copy(a, b, s_small.at[n])
        for n, (a, b) in enumerate(((diel_in, diel), (owner_in, owner), (slots_in, slots)))
    ]
    for p in ORDER:
        loads[p].start()
    for copy in small:
        copy.start()

    barrier = pltpu.get_barrier_semaphore()
    for dg in range(GROUPS):
        for dc in range(2):
            if dg or dc:
                to = (lax.rem(g + dg, GROUPS), gx, 2 * zl + (c if dc == 0 else 1 - c))
                pl.semaphore_signal(barrier, inc=1, device_id=to, device_id_type=MESH)
    across = (g, gx, lax.rem(gy + 3 + 2 * c, 4))
    for to in (left, right, across):
        pl.semaphore_signal(barrier, inc=1, device_id=to, device_id_type=MESH)
    for copy in loads + small:
        copy.wait()
    pl.semaphore_wait(barrier, 10)

    def pack_ends(f, carry):
        for x in range(XS):
            ys[0, f, 2 * x : 2 * x + 2, :] = orb[f, x, 0:2, :]
            ys[1, f, 2 * x : 2 * x + 2, :] = orb[f, x, 38:40, :]
        return carry

    lax.fori_loop(0, RES, pack_ends, 0)
    for x in range(XS):
        ys[0, RES, 2 * x : 2 * x + 2, :] = diel[x, 0:2, :]
        ys[1, RES, 2 * x : 2 * x + 2, :] = diel[x, 38:40, :]
    to_down = remote(ys.at[0], yr.at[1], s_y.at[0], r_y.at[1], down)
    to_up = remote(ys.at[1], yr.at[0], s_y.at[1], r_y.at[0], up)
    to_down.start()
    to_up.start()

    def pack(p, which):
        def body(f, carry):
            for xx in range(2):
                x = 2 * p + xx
                at = pl.multiple_of(24 * f, 8)
                for wi in which:
                    o = 12 * xx
                    if wi == 0:
                        send[p, wi, f, o : o + 2, :] = yr[0, f, 2 * x : 2 * x + 2, :]
                        send[p, wi, f, o + 2 : o + 12, :] = orb[f, x, 0:10, :]
                    elif wi == 3:
                        send[p, wi, f, o : o + 10, :] = orb[f, x, 30:40, :]
                        send[p, wi, f, o + 10 : o + 12, :] = yr[1, f, 2 * x : 2 * x + 2, :]
                    else:
                        send[p, wi, f, o : o + 12, :] = orb[f, x, STARTS[wi] : STARTS[wi] + 12, :]
            return carry

        lax.fori_loop(0, RES, body, 0)

    def share_copy(p, wi):
        to = (2 * c + wi // 2, gx, 2 * zl + wi % 2)
        here = jnp.logical_and(to[0] == g, c == wi % 2)
        away = remote(send.at[p, wi], rb.at[p + 1, g], s_send.at[p, wi], r_send.at[p, g], to)
        near = pltpu.make_async_copy(send.at[p, wi], rb.at[p + 1, g], l_send.at[p])
        return here, away, near

    def share_start(p, wi):
        here, away, near = share_copy(p, wi)
        pl.when(here)(near.start)
        pl.when(jnp.logical_not(here))(away.start)

    def share_sent(p, wi):
        here, away, near = share_copy(p, wi)
        pl.when(jnp.logical_not(here))(away.wait_send)

    def share_arrived(p, source):
        near_one = jnp.logical_and(g == source, mine)
        near = pltpu.make_async_copy(send.at[p, 0], rb.at[p + 1, source], l_send.at[p])
        away = remote(send.at[p, 0], rb.at[p + 1, source], s_send.at[p, 0], r_send.at[p, source], sibling)
        pl.when(near_one)(near.wait)
        pl.when(jnp.logical_not(near_one))(away.wait_recv)

    for p in ORDER[:2]:
        pack(p, (1, 2))
        share_start(p, 1)
        share_start(p, 2)
    to_down.wait()
    to_up.wait()
    for p in ORDER[:2]:
        pack(p, (0, 3))
        share_start(p, 0)
        share_start(p, 3)

    for ch in range(2):
        for ph in range(2):

            @pl.when(jnp.logical_and(mine, jnp.logical_and(c == ch, part == ph)))
            def _():
                for k in range(2):
                    wi = 2 * ph + k
                    for x in range(XS):
                        p, o = x // 2, ROW * (x % 2)
                        if wi == 0:
                            ds_[k, p, o : o + 2, :] = yr[0, RES, 2 * x : 2 * x + 2, :]
                            ds_[k, p, o + 2 : o + 14, :] = diel[x, 0:12, :]
                        elif wi == 3:
                            ds_[k, p, o : o + 12, :] = diel[x, 28:40, :]
                            ds_[k, p, o + 12 : o + 14, :] = yr[1, RES, 2 * x : 2 * x + 2, :]
                        else:
                            ds_[k, p, o : o + 14, :] = diel[x, 10 * wi - 2 : 10 * wi + 12, :]
                near = pltpu.make_async_copy(ds_.at[ch], db.at[pl.ds(1, PAIRS)], l_d)
                away = remote(ds_.at[1 - ch], db.at[pl.ds(1, PAIRS)], s_d, r_d, sibling)
                near.start()
                away.start()
                near.wait()
                away.wait_send()

    for p in ORDER[2:]:
        pack(p, (0, 1, 2, 3))
        for wi in range(4):
            share_start(p, wi)

    @pl.when(jnp.logical_not(mine))
    def _():
        remote(ds_.at[0], db.at[pl.ds(1, PAIRS)], s_d, r_d, sibling).wait_recv()

    d_left = remote(db.at[1], db.at[6], s_dx.at[0], r_dx.at[0], left)
    d_right = remote(db.at[5], db.at[0], s_dx.at[1], r_dx.at[1], right)
    d_left.start()
    d_right.start()
    d_left.wait()
    d_right.wait()
    wd[...] = jnp.zeros_like(wd)
    for s in range(7):
        wd[BASE + 28 * s : BASE + 28 * s + 28, :] = db[s, 0:28, :]

    lane = lax.broadcasted_iota(jnp.int32, (8, 128), 1)
    top, bottom = lane == 127, lane == 0

    def ahead(v, n=1):
        return pltpu.roll(v, 128 - n, 1)

    def at(ref, r, n=0):
        return ref[r + n : r + n + 8, :]

    for i in range(29):
        r = 8 * i
        if r + 14 + 8 > ROWS:
            break
        e, ex, ey = at(wd, r), at(wd, r, 14), at(wd, r, 1)
        kx[r : r + 8, :] = 0.5 * (e + ex)
        ky[r : r + 8, :] = 0.5 * (e + ey)
        kz[r : r + 8, :] = jnp.where(top, 0.0, 0.5 * (e + ahead(e)))

    def squared(r):
        e = at(wd, r)
        x1, x0, y1, y0 = at(kx, r), at(kx, r, -14), at(ky, r), at(ky, r, -1)
        z1 = at(kz, r)
        z0 = pltpu.roll(z1, 1, 1)
        ends = jnp.where(jnp.logical_or(top, bottom), e, 0.0)
        total = x1 + x0 + y1 + y0 + z1 + z0 + ends
        squares = x1 * x1 + x0 * x0 + y1 * y1 + y0 * y0 + z1 * z1 + z0 * z0
        return total, squares

    for i in range(2, 27):
        r = 8 * i
        total, squares = squared(r)
        dd[0, r : r + 8, :] = total
        dd[1, r : r + 8, :] = squares

    def couplings(k):
        r = FIRST + 8 * k
        d0, sq = at(dd.at[0], r), at(dd.at[1], r)
        x1, y1, z1 = at(kx, r), at(ky, r), at(kz, r)
        dx, dy = at(dd.at[0], r, 14), at(dd.at[0], r, 1)
        xx, yx, zx = at(kx, r, 14), at(ky, r, 14), at(kz, r, 14)
        xy, yy, zy = at(kx, r, 1), at(ky, r, 1), at(kz, r, 1)
        dz, xz, yz, zz = ahead(d0), ahead(x1), ahead(y1), ahead(z1)
        values = (
            C0 + C1 * d0 + C2 * (d0 * d0 + sq),
            -x1 * (C1 + C2 * (d0 + dx)),
            -y1 * (C1 + C2 * (d0 + dy)),
            -z1 * (C1 + C2 * (d0 + dz)),
            C2 * (x1 * xx),
            C2 * (y1 * yy),
            C2 * (z1 * zz),
            C2 * (x1 * yx + y1 * xy),
            C2 * (x1 * y1 + xy * yx),
            C2 * (x1 * zx + z1 * xz),
            C2 * (x1 * z1 + xz * zx),
            C2 * (y1 * zy + z1 * yz),
            C2 * (y1 * z1 + yz * zy),
        )
        for n, v in enumerate(values):
            coup[n, LEAD + 8 * k : LEAD + 8 * k + 8, :] = v

    for k in range(-LEAD_CHUNKS, CHUNKS):
        couplings(k)

    def sib_copy(p):
        return remote(sib_s.at[p], sib_r.at[p + 1], s_sib.at[p], r_sib.at[p], sibling)

    def arrive(p):
        for source in range(GROUPS):
            share_arrived(p, source)
        for ch in range(2):

            @pl.when(c == ch)
            def _():
                def body(o, carry):
                    q, f = o // RES, lax.rem(o, RES)
                    for xx in range(2):
                        a = 12 * xx + (10 if ch == 0 else 0)
                        sib_s[p, o, 2 * xx : 2 * xx + 2, :] = rb[p + 1, q, f, a : a + 2, :]
                    return carry

                lax.fori_loop(0, ORBS, body, 0)

        sib_copy(p).start()

    def edge_copies(p):
        to, slot, n = (left, 6, 0) if p == 0 else (right, 0, 1)
        return (
            remote(rb.at[p + 1], rb.at[slot], s_x.at[n], r_x.at[n], to),
            remote(sib_r.at[p + 1], sib_r.at[slot], s_xs.at[n], r_xs.at[n], to),
        )

    def unpack(slot):
        for ch in range(2):

            @pl.when(c == ch)
            def _():
                def body(o, carry):
                    q, f = o // RES, lax.rem(o, RES)
                    for xx in range(2):
                        r = BASE + 28 * slot + ROW * xx
                        m = r + (0 if ch == 0 else 2)
                        h = r + (12 if ch == 0 else 0)
                        w[o, m : m + 12, :] = rb[slot, q, f, 12 * xx : 12 * xx + 12, :]
                        w[o, h : h + 2, :] = sib_r[slot, o, 2 * xx : 2 * xx + 2, :]
                    return carry

                lax.fori_loop(0, ORBS, body, 0, unroll=2)

        def turn(o, carry):
            for n in range(4):
                r = BASE + 28 * slot + 8 * n
                v = w[o, r : r + 8, :]
                wz[o, r : r + 8, :] = ahead(v)
                wz2[o, r : r + 8, :] = ahead(v, 2)
            return carry

        lax.fori_loop(0, ORBS, turn, 0, unroll=4)

    def density(k, carry):
        r = pl.multiple_of(FIRST - LEAD + 8 * k, 8)
        d = pl.multiple_of(8 * k, 8)

        def body(i, acc):
            for n in range(4):
                o = 4 * i + n

                def row(ref, shift=0):
                    return ref[o, pl.ds(r + shift, 8), :]

                a, b, b2 = row(w), row(w, 14), row(w, 28)
                y1, y2, xy = row(w, 1), row(w, 2), row(w, 15)
                az, az2, bz, yz = row(wz), row(wz2), row(wz, 14), row(wz, 1)
                terms = (
                    a * a, a * b, a * y1, a * az, a * b2, a * y2, a * az2,
                    a * xy, b * y1, a * bz, az * b, a * yz, az * y1,
                )
                acc = tuple(s + t for s, t in zip(acc, terms))
            return acc

        acc = lax.fori_loop(0, ORBS // 4, body, (jnp.zeros((8, 128), F32),) * 13)
        for n in range(13):
            dens[n, pl.ds(d, 8), :] = coup[n, pl.ds(d, 8), :] * acc[n]
        return carry

    chosen = [owner[n // 4] * RES + slots[n // 4, n % 4] for n in range(8)]

    def apply(k, carry):
        r = pl.multiple_of(FIRST + 8 * k, 8)
        d = pl.multiple_of(LEAD + 8 * k, 8)

        def m(n, back=0):
            return dens[n, pl.ds(d - back, 8), :]

        level = (
            (0, m(0)), (14, m(1)), (-14, m(1, 14)), (1, m(2)), (-1, m(2, 1)), (28, m(4)), (-28, m(4, 28)),
            (2, m(5)), (-2, m(5, 2)), (15, m(7)), (-15, m(7, 15)), (13, m(8, 1)), (-13, m(8, 14)),
        )
        z1, z2 = m(3), m(6)
        lower = ((0, z1), (14, m(10)), (-14, m(9, 14)), (1, m(12)), (-1, m(11, 1)))
        upper = ((0, z1), (14, m(9)), (-14, m(10, 14)), (1, m(11)), (-1, m(12, 1)))
        for n in range(8):
            o = chosen[n]
            v = {s: w[o, pl.ds(r + s, 8), :] for s, _ in level}

            def total(terms):
                while len(terms) > 1:
                    terms = [sum(terms[i + 1 : i + 2], terms[i]) for i in range(0, len(terms), 2)]
                return terms[0]

            below = total([x * v[s] for s, x in lower])
            res = total(
                [x * v[s] for s, x in level]
                + [x * wz[o, pl.ds(r + s, 8), :] for s, x in upper]
                + [z2 * wz2[o, pl.ds(r, 8), :]]
            )
            res = res + pltpu.roll(below, 1, 1) + pltpu.roll(z2 * v[0], 2, 1)
            flat[n, pl.ds(pl.multiple_of(8 * k, 8), 8), :] = res
        return carry

    def out_copy(piece, j):
        to = (j, gx, 2 * zl + home)
        here = jnp.logical_and(g == j, mine)
        slot = 2 * part + c
        source, target = (ob0, ob1, ob2)[piece], (or0, or1, or2)[piece]
        away = remote(source.at[j], target.at[slot], s_o.at[piece, j], r_o.at[piece, slot], to)
        near = pltpu.make_async_copy(source.at[j], target.at[slot], l_o.at[piece])
        return here, away, near

    def out_start(piece):
        first, count = PIECES[piece]
        source = (ob0, ob1, ob2)[piece]

        def pack_out(j, carry):
            for window in range(2):
                for n in range(count):
                    o, x = 10 * (count * window + n), first + n
                    source[j, o : o + 10, :] = flat[4 * window + j, ROW * x : ROW * x + 10, :]
            return carry

        lax.fori_loop(0, GROUPS, pack_out, 0)
        for j in range(GROUPS):
            here, away, near = out_copy(piece, j)
            pl.when(here)(near.start)
            pl.when(jnp.logical_not(here))(away.start)

    def out_place(piece):
        first, count = PIECES[piece]
        source, target = (ob0, ob1, ob2)[piece], (or0, or1, or2)[piece]
        for wi in range(4):
            here = jnp.logical_and(2 * c + wi // 2 == g, c == wi % 2)
            away = remote(source.at[0], target.at[wi], s_o.at[piece, 0], r_o.at[piece, wi], sibling)
            near = pltpu.make_async_copy(source.at[0], target.at[wi], l_o.at[piece])
            pl.when(here)(near.wait)
            pl.when(jnp.logical_not(here))(away.wait_recv)
            for window in range(2):
                for n in range(count):
                    o = 10 * (count * window + n)
                    out[window, 0, first + n, 10 * wi : 10 * wi + 10, :] = target[wi, o : o + 10, :]

    for p in (0, 4):
        arrive(p)
        edge_copies(p)[0].start()
    for p in (0, 4):
        sib_copy(p).wait()
        edge_copies(p)[1].start()
        unpack(p + 1)
    arrive(1)
    sib_copy(1).wait()
    unpack(2)
    for p in (0, 4):
        for e in edge_copies(p):
            e.wait()
    unpack(0)
    unpack(6)
    lax.fori_loop(0, 7, density, 0)
    lax.fori_loop(0, 3, apply, 0)
    out_start(0)
    arrive(3)
    sib_copy(3).wait()
    unpack(4)
    lax.fori_loop(14, 21, density, 0)
    lax.fori_loop(14, 17, apply, 0)
    out_start(1)
    arrive(2)
    sib_copy(2).wait()
    unpack(3)
    lax.fori_loop(7, 15, density, 0)
    lax.fori_loop(3, 14, apply, 0)
    out_start(2)
    for piece in range(3):
        out_place(piece)

    for p in range(PAIRS):
        for wi in range(4):
            share_sent(p, wi)
    for piece in range(3):
        for j in range(GROUPS):
            here, away, near = out_copy(piece, j)
            pl.when(jnp.logical_not(here))(away.wait_send)


def shards(orbitals, dielectric, owner_group, block_slots):
    dma = pltpu.SemaphoreType.DMA
    vmem = pl.BlockSpec(memory_space=pltpu.VMEM)

    def buf(*shape):
        return pltpu.VMEM(shape + (128,), F32)

    return pl.pallas_call(
        kernel,
        out_shape=jax.ShapeDtypeStruct((2, 1, 10, 40, 128), F32),
        in_specs=[pl.BlockSpec(memory_space=pl.ANY)] * 4,
        out_specs=vmem,
        scratch_shapes=[
            buf(RES, XS, 40), buf(XS, 40), pltpu.SMEM((2,), jnp.int32), pltpu.SMEM((2, 4), jnp.int32),
            dma((PAIRS,)), dma((3,)),
            buf(PAIRS, 4, RES, 24), buf(7, GROUPS, RES, 24), buf(PAIRS, ORBS, 8), buf(7, ORBS, 8),
            buf(2, RES + 1, 24), buf(2, RES + 1, 24), buf(2, PAIRS, 32), buf(7, 32),
            buf(ORBS, ROWS), buf(ORBS, ROWS), buf(ORBS, ROWS),
            buf(ROWS), buf(ROWS), buf(ROWS), buf(ROWS), buf(2, ROWS),
            buf(13, COUP), buf(13, COUP), buf(8, CHUNKS * 8),
            buf(GROUPS, 40), buf(GROUPS, 40), buf(GROUPS, 120), buf(4, 40), buf(4, 40), buf(4, 120),
            dma((PAIRS, 4)), dma((PAIRS, 4)), dma((PAIRS,)),
            dma((PAIRS,)), dma((PAIRS,)), dma((2,)), dma((2,)), dma((2,)), dma((2,)), dma((2,)), dma((2,)),
            dma, dma, dma, dma((2,)), dma((2,)), dma((3, GROUPS)), dma((3, 4)), dma((3,)),
        ],
        compiler_params=pltpu.CompilerParams(collective_id=0, has_side_effects=True, vmem_limit_bytes=60 << 20),
        cost_estimate=pl.CostEstimate(flops=60_000_000, bytes_accessed=2_500_000, transcendentals=0),
    )(orbitals, dielectric, owner_group, block_slots)


def solution(mesh):
    in_specs = (P("orb", "gx", "gy", None), P("gx", "gy", None), P(), P())
    out_specs = P(None, "orb", "gx", "gy", None)
    return jax.shard_map(shards, mesh=mesh, in_specs=in_specs, out_specs=out_specs, check_vma=False)
```

```python
import math

import jax
import jax.numpy as jnp
from jax import lax
from jax.experimental import pallas as pl
from jax.experimental.pallas import tpu as pltpu
from jax.sharding import PartitionSpec as P

MESH = pl.DeviceIdType.MESH
F32 = jnp.float32

MIXING = 0.25
LOWEST = 0.5
HIGHEST = 24.0
MID = (HIGHEST + LOWEST) / 2.0
HALF = (HIGHEST - LOWEST) / 2.0
RATIO = MID / HALF
R0 = 1.0 / RATIO
R1 = 1.0 / (2.0 * RATIO - R0)
R2 = 1.0 / (2.0 * RATIO - R1)
K1, K2 = R1 * R0, R2 * R1
S1, S2 = 2.0 * R1 / HALF, 2.0 * R2 / HALF
Q = 1.0 / MID
ALPHA, BETA = K1 * Q + S1, S1 * Q
SCALE = -MIXING * 4.0 * math.pi
C0 = SCALE * (Q + ALPHA + K2 * ALPHA + S2)
C1 = -SCALE * (BETA + K2 * BETA + S2 * (Q + ALPHA))
C2 = SCALE * S2 * BETA

GROUPS = 4
RES = 8
ORBS = 32
XS = 10
SUB = 10
ROW = 14
PAIRS = 5
BASE = 18
FIRST = BASE + 2 * ROW + 2
LEAD = 32
ROWS = 240
CHUNKS = 17
LEAD_CHUNKS = 4
COUP = (CHUNKS + LEAD_CHUNKS) * 8
STARTS = (-2, 10, 18, 30)
ORDER = (0, 4, 1, 3, 2)
PIECES = (0, 8, 2, 4, 6)


def kernel(
    orb_in, diel_in, owner_in, slots_in, out,
    orb, diel, owner, slots, s_in, s_small, send, rb, sib_s, sib_r, ys, yr, ds_, db, w, wz, wz2, wd, kx, ky, kz, dd, coup, dens, flat, ob, orr,
    s_send, r_send, l_send, s_sib, r_sib, s_y, r_y, s_x, r_x, s_xs, r_xs, s_d, r_d, l_d, s_dx, r_dx, s_o, r_o, l_o,
):
    g, gx, gy = lax.axis_index("orb"), lax.axis_index("gx"), lax.axis_index("gy")
    zl, c = gy // 2, lax.rem(gy, 2)
    home = g // 2
    mine = c == home
    part = lax.rem(g, 2)
    sibling = (g, gx, 2 * zl + 1 - c)
    left, right = (g, lax.rem(gx + 15, 16), gy), (g, lax.rem(gx + 1, 16), gy)
    down, up = (g, gx, lax.rem(gy + 3, 4)), (g, gx, lax.rem(gy + 1, 4))

    def remote(src, dst, ss, rs, to):
        return pltpu.make_async_remote_copy(
            src_ref=src, dst_ref=dst, send_sem=ss, recv_sem=rs, device_id=to, device_id_type=MESH
        )

    loads = [
        pltpu.make_async_copy(orb_in.at[:, pl.ds(2 * p, 2)], orb.at[:, pl.ds(2 * p, 2)], s_in.at[p]) for p in range(PAIRS)
    ]
    small = [
        pltpu.make_async_copy(a, b, s_small.at[n])
        for n, (a, b) in enumerate(((diel_in, diel), (owner_in, owner), (slots_in, slots)))
    ]
    for p in ORDER:
        loads[p].start()
    for copy in small:
        copy.start()

    barrier = pltpu.get_barrier_semaphore()
    for dg in range(GROUPS):
        for dc in range(2):
            if dg or dc:
                to = (lax.rem(g + dg, GROUPS), gx, 2 * zl + (c if dc == 0 else 1 - c))
                pl.semaphore_signal(barrier, inc=1, device_id=to, device_id_type=MESH)
    across = (g, gx, lax.rem(gy + 3 + 2 * c, 4))
    for to in (left, right, across):
        pl.semaphore_signal(barrier, inc=1, device_id=to, device_id_type=MESH)

    def pack(p, which):
        def body(f, carry):
            for xx in range(2):
                x = 2 * p + xx
                at = pl.multiple_of(24 * f, 8)
                for wi in which:
                    o = 12 * xx
                    if wi == 0:
                        send[p, wi, f, o : o + 2, :] = yr[0, f, 2 * x : 2 * x + 2, :]
                        send[p, wi, f, o + 2 : o + 12, :] = orb[f, x, 0:10, :]
                    elif wi == 3:
                        send[p, wi, f, o : o + 10, :] = orb[f, x, 30:40, :]
                        send[p, wi, f, o + 10 : o + 12, :] = yr[1, f, 2 * x : 2 * x + 2, :]
                    else:
                        send[p, wi, f, o : o + 12, :] = orb[f, x, STARTS[wi] : STARTS[wi] + 12, :]
            return carry

        lax.fori_loop(0, RES, body, 0)

    def share_copy(p, wi):
        to = (2 * c + wi // 2, gx, 2 * zl + wi % 2)
        here = jnp.logical_and(to[0] == g, c == wi % 2)
        away = remote(send.at[p, wi], rb.at[p + 1, g], s_send.at[p, wi], r_send.at[p, g], to)
        near = pltpu.make_async_copy(send.at[p, wi], rb.at[p + 1, g], l_send.at[p])
        return here, away, near

    def share_start(p, wi):
        here, away, near = share_copy(p, wi)
        pl.when(here)(near.start)
        pl.when(jnp.logical_not(here))(away.start)

    def share_sent(p, wi):
        here, away, near = share_copy(p, wi)
        pl.when(jnp.logical_not(here))(away.wait_send)

    def share_arrived(p, source):
        near_one = jnp.logical_and(g == source, mine)
        near = pltpu.make_async_copy(send.at[p, 0], rb.at[p + 1, source], l_send.at[p])
        away = remote(send.at[p, 0], rb.at[p + 1, source], s_send.at[p, 0], r_send.at[p, source], sibling)
        pl.when(near_one)(near.wait)
        pl.when(jnp.logical_not(near_one))(away.wait_recv)

    loads[0].wait()
    pack(0, (1, 2))
    pl.semaphore_wait(barrier, 10)
    share_start(0, 1)
    share_start(0, 2)
    for copy in loads[1:] + small:
        copy.wait()

    def pack_ends(f, carry):
        for x in range(XS):
            ys[0, f, 2 * x : 2 * x + 2, :] = orb[f, x, 0:2, :]
            ys[1, f, 2 * x : 2 * x + 2, :] = orb[f, x, 38:40, :]
        return carry

    lax.fori_loop(0, RES, pack_ends, 0)
    for x in range(XS):
        ys[0, RES, 2 * x : 2 * x + 2, :] = diel[x, 0:2, :]
        ys[1, RES, 2 * x : 2 * x + 2, :] = diel[x, 38:40, :]
    to_down = remote(ys.at[0], yr.at[1], s_y.at[0], r_y.at[1], down)
    to_up = remote(ys.at[1], yr.at[0], s_y.at[1], r_y.at[0], up)
    to_down.start()
    to_up.start()

    pack(4, (1, 2))
    share_start(4, 1)
    share_start(4, 2)
    to_down.wait()
    to_up.wait()
    for ch in range(2):
        for ph in range(2):

            @pl.when(jnp.logical_and(mine, jnp.logical_and(c == ch, part == ph)))
            def _():
                for k in range(2):
                    wi = 2 * ph + k
                    for x in range(XS):
                        p, o = x // 2, ROW * (x % 2)
                        if wi == 0:
                            ds_[k, p, o : o + 2, :] = yr[0, RES, 2 * x : 2 * x + 2, :]
                            ds_[k, p, o + 2 : o + 14, :] = diel[x, 0:12, :]
                        elif wi == 3:
                            ds_[k, p, o : o + 12, :] = diel[x, 28:40, :]
                            ds_[k, p, o + 12 : o + 14, :] = yr[1, RES, 2 * x : 2 * x + 2, :]
                        else:
                            ds_[k, p, o : o + 14, :] = diel[x, 10 * wi - 2 : 10 * wi + 12, :]
                near = pltpu.make_async_copy(ds_.at[ch], db.at[pl.ds(1, PAIRS)], l_d)
                away = remote(ds_.at[1 - ch], db.at[pl.ds(1, PAIRS)], s_d, r_d, sibling)
                near.start()
                away.start()

    for p in ORDER[:2]:
        pack(p, (0, 3))
        share_start(p, 0)
        share_start(p, 3)

    for p in ORDER[2:]:
        pack(p, (0, 1, 2, 3))

    @pl.when(mine)
    def _():
        pltpu.make_async_copy(ds_.at[0], db.at[pl.ds(1, PAIRS)], l_d).wait()
        remote(ds_.at[0], db.at[pl.ds(1, PAIRS)], s_d, r_d, sibling).wait_send()

    @pl.when(jnp.logical_not(mine))
    def _():
        remote(ds_.at[0], db.at[pl.ds(1, PAIRS)], s_d, r_d, sibling).wait_recv()

    d_left = remote(db.at[1], db.at[6], s_dx.at[0], r_dx.at[0], left)
    d_right = remote(db.at[5], db.at[0], s_dx.at[1], r_dx.at[1], right)
    d_left.start()
    d_right.start()

    def sib_copy(p):
        return remote(sib_s.at[p], sib_r.at[p + 1], s_sib.at[p], r_sib.at[p], sibling)

    def arrive(p):
        for source in range(GROUPS):
            share_arrived(p, source)
        for ch in range(2):

            @pl.when(c == ch)
            def _():
                def body(o, carry):
                    q, f = o // RES, lax.rem(o, RES)
                    for xx in range(2):
                        a = 12 * xx + (10 if ch == 0 else 0)
                        sib_s[p, o, 2 * xx : 2 * xx + 2, :] = rb[p + 1, q, f, a : a + 2, :]
                    return carry

                lax.fori_loop(0, ORBS, body, 0)

        sib_copy(p).start()

    def edge_copies(p):
        to, slot, n = (left, 6, 0) if p == 0 else (right, 0, 1)
        return (
            remote(rb.at[p + 1], rb.at[slot], s_x.at[n], r_x.at[n], to),
            remote(sib_r.at[p + 1], sib_r.at[slot], s_xs.at[n], r_xs.at[n], to),
        )

    def unpack(slot):
        for ch in range(2):

            @pl.when(c == ch)
            def _():
                def body(o, carry):
                    q, f = o // RES, lax.rem(o, RES)
                    for xx in range(2):
                        r = BASE + 28 * slot + ROW * xx
                        m = r + (0 if ch == 0 else 2)
                        h = r + (12 if ch == 0 else 0)
                        w[o, m : m + 12, :] = rb[slot, q, f, 12 * xx : 12 * xx + 12, :]
                        w[o, h : h + 2, :] = sib_r[slot, o, 2 * xx : 2 * xx + 2, :]
                    return carry

                lax.fori_loop(0, ORBS, body, 0, unroll=2)

        def turn(o, carry):
            for n in range(4):
                r = BASE + 28 * slot + 8 * n
                v = w[o, r : r + 8, :]
                wz[o, r : r + 8, :] = ahead(v)
                wz2[o, r : r + 8, :] = ahead(v, 2)
            return carry

        lax.fori_loop(0, ORBS, turn, 0, unroll=4)

    def density(k, carry):
        r = pl.multiple_of(FIRST - LEAD + 8 * k, 8)
        d = pl.multiple_of(8 * k, 8)

        def body(i, acc):
            for n in range(4):
                o = 4 * i + n

                def row(ref, shift=0):
                    return ref[o, pl.ds(r + shift, 8), :]

                a, b, b2 = row(w), row(w, 14), row(w, 28)
                y1, y2, xy = row(w, 1), row(w, 2), row(w, 15)
                az, az2, bz, yz = row(wz), row(wz2), row(wz, 14), row(wz, 1)
                terms = (
                    a * a, a * b, a * y1, a * az, a * b2, a * y2, a * az2,
                    a * xy, b * y1, a * bz, az * b, a * yz, az * y1,
                )
                acc = tuple(s + t for s, t in zip(acc, terms))
            return acc

        acc = lax.fori_loop(0, ORBS // 4, body, (jnp.zeros((8, 128), F32),) * 13)
        for n in range(13):
            dens[n, pl.ds(d, 8), :] = coup[n, pl.ds(d, 8), :] * acc[n]
        return carry

    chosen = [owner[n // 4] * RES + slots[n // 4, n % 4] for n in range(8)]

    def apply(k, carry):
        r = pl.multiple_of(FIRST + 8 * k, 8)
        d = pl.multiple_of(LEAD + 8 * k, 8)

        def m(n, back=0):
            return dens[n, pl.ds(d - back, 8), :]

        level = (
            (0, m(0)), (14, m(1)), (-14, m(1, 14)), (1, m(2)), (-1, m(2, 1)), (28, m(4)), (-28, m(4, 28)),
            (2, m(5)), (-2, m(5, 2)), (15, m(7)), (-15, m(7, 15)), (13, m(8, 1)), (-13, m(8, 14)),
        )
        z1, z2 = m(3), m(6)
        lower = ((0, z1), (14, m(10)), (-14, m(9, 14)), (1, m(12)), (-1, m(11, 1)))
        upper = ((0, z1), (14, m(9)), (-14, m(10, 14)), (1, m(11)), (-1, m(12, 1)))
        for n in range(8):
            o = chosen[n]
            v = {s: w[o, pl.ds(r + s, 8), :] for s, _ in level}

            def total(terms):
                while len(terms) > 1:
                    terms = [sum(terms[i + 1 : i + 2], terms[i]) for i in range(0, len(terms), 2)]
                return terms[0]

            below = total([x * v[s] for s, x in lower])
            res = total(
                [x * v[s] for s, x in level]
                + [x * wz[o, pl.ds(r + s, 8), :] for s, x in upper]
                + [z2 * wz2[o, pl.ds(r, 8), :]]
            )
            res = res + pltpu.roll(below, 1, 1) + pltpu.roll(z2 * v[0], 2, 1)
            flat[n, pl.ds(pl.multiple_of(8 * k, 8), 8), :] = res
        return carry

    def out_copy(piece, j):
        to = (j, gx, 2 * zl + home)
        here = jnp.logical_and(g == j, mine)
        slot = 2 * part + c
        source, target = ob.at[piece], orr.at[piece]
        away = remote(source.at[j], target.at[slot], s_o.at[piece, j], r_o.at[piece, slot], to)
        near = pltpu.make_async_copy(source.at[j], target.at[slot], l_o.at[piece])
        return here, away, near

    def out_start(piece):
        first = PIECES[piece]

        def pack_out(j, carry):
            for window in range(2):
                for n in range(2):
                    o, x = 10 * (2 * window + n), first + n
                    ob[piece, j, o : o + 10, :] = flat[4 * window + j, ROW * x : ROW * x + 10, :]
            return carry

        lax.fori_loop(0, GROUPS, pack_out, 0)
        for j in range(GROUPS):
            here, away, near = out_copy(piece, j)
            pl.when(here)(near.start)
            pl.when(jnp.logical_not(here))(away.start)

    def out_place(piece):
        first = PIECES[piece]
        source, target = ob.at[piece], orr.at[piece]
        for wi in range(4):
            here = jnp.logical_and(2 * c + wi // 2 == g, c == wi % 2)
            away = remote(source.at[0], target.at[wi], s_o.at[piece, 0], r_o.at[piece, wi], sibling)
            near = pltpu.make_async_copy(source.at[0], target.at[wi], l_o.at[piece])
            pl.when(here)(near.wait)
            pl.when(jnp.logical_not(here))(away.wait_recv)
            for window in range(2):
                for n in range(2):
                    o = 10 * (2 * window + n)
                    out[window, 0, first + n, 10 * wi : 10 * wi + 10, :] = target[wi, o : o + 10, :]

    def follow(p, later):
        for wi in range(4):
            share_sent(p, wi)
        for wi in range(4):
            share_start(later, wi)

    for p, later in ((0, 1), (4, 3)):
        arrive(p)
        edge_copies(p)[0].start()
        follow(p, later)

    d_left.wait()
    d_right.wait()
    wd[...] = jnp.zeros_like(wd)
    for s in range(7):
        wd[BASE + 28 * s : BASE + 28 * s + 28, :] = db[s, 0:28, :]

    lane = lax.broadcasted_iota(jnp.int32, (8, 128), 1)
    top, bottom = lane == 127, lane == 0

    def ahead(v, n=1):
        return pltpu.roll(v, 128 - n, 1)

    def at(ref, r, n=0):
        return ref[r + n : r + n + 8, :]

    for i in range(29):
        r = 8 * i
        if r + 14 + 8 > ROWS:
            break
        e, ex, ey = at(wd, r), at(wd, r, 14), at(wd, r, 1)
        kx[r : r + 8, :] = 0.5 * (e + ex)
        ky[r : r + 8, :] = 0.5 * (e + ey)
        kz[r : r + 8, :] = jnp.where(top, 0.0, 0.5 * (e + ahead(e)))

    def squared(r):
        e = at(wd, r)
        x1, x0, y1, y0 = at(kx, r), at(kx, r, -14), at(ky, r), at(ky, r, -1)
        z1 = at(kz, r)
        z0 = pltpu.roll(z1, 1, 1)
        ends = jnp.where(jnp.logical_or(top, bottom), e, 0.0)
        total = x1 + x0 + y1 + y0 + z1 + z0 + ends
        squares = x1 * x1 + x0 * x0 + y1 * y1 + y0 * y0 + z1 * z1 + z0 * z0
        return total, squares

    for i in range(2, 27):
        r = 8 * i
        total, squares = squared(r)
        dd[0, r : r + 8, :] = total
        dd[1, r : r + 8, :] = squares

    def couplings(k):
        r = FIRST + 8 * k
        d0, sq = at(dd.at[0], r), at(dd.at[1], r)
        x1, y1, z1 = at(kx, r), at(ky, r), at(kz, r)
        dx, dy = at(dd.at[0], r, 14), at(dd.at[0], r, 1)
        xx, yx, zx = at(kx, r, 14), at(ky, r, 14), at(kz, r, 14)
        xy, yy, zy = at(kx, r, 1), at(ky, r, 1), at(kz, r, 1)
        dz, xz, yz, zz = ahead(d0), ahead(x1), ahead(y1), ahead(z1)
        values = (
            C0 + C1 * d0 + C2 * (d0 * d0 + sq),
            -x1 * (C1 + C2 * (d0 + dx)),
            -y1 * (C1 + C2 * (d0 + dy)),
            -z1 * (C1 + C2 * (d0 + dz)),
            C2 * (x1 * xx),
            C2 * (y1 * yy),
            C2 * (z1 * zz),
            C2 * (x1 * yx + y1 * xy),
            C2 * (x1 * y1 + xy * yx),
            C2 * (x1 * zx + z1 * xz),
            C2 * (x1 * z1 + xz * zx),
            C2 * (y1 * zy + z1 * yz),
            C2 * (y1 * z1 + yz * zy),
        )
        for n, v in enumerate(values):
            coup[n, LEAD + 8 * k : LEAD + 8 * k + 8, :] = v

    for k in range(-LEAD_CHUNKS, CHUNKS):
        couplings(k)

    for p in (0, 4):
        sib_copy(p).wait()
        edge_copies(p)[1].start()
        unpack(p + 1)
    arrive(1)
    follow(1, 2)
    sib_copy(1).wait()
    unpack(2)
    for p in (0, 4):
        for e in edge_copies(p):
            e.wait()
    unpack(0)
    unpack(6)
    lax.fori_loop(0, 7, density, 0)
    lax.fori_loop(0, 3, apply, 0)
    out_start(0)
    arrive(3)
    sib_copy(3).wait()
    unpack(4)
    lax.fori_loop(14, 21, density, 0)
    lax.fori_loop(14, 17, apply, 0)
    out_start(1)
    arrive(2)
    sib_copy(2).wait()
    unpack(3)
    lax.fori_loop(7, 11, density, 0)
    lax.fori_loop(3, 7, apply, 0)
    out_start(2)
    lax.fori_loop(11, 14, density, 0)
    lax.fori_loop(7, 10, apply, 0)
    out_start(3)
    lax.fori_loop(14, 15, density, 0)
    lax.fori_loop(10, 14, apply, 0)
    out_start(4)
    for piece in range(len(PIECES)):
        out_place(piece)

    for p in (3, 2):
        for wi in range(4):
            share_sent(p, wi)
    for piece in range(len(PIECES)):
        for j in range(GROUPS):
            here, away, near = out_copy(piece, j)
            pl.when(jnp.logical_not(here))(away.wait_send)


def shards(orbitals, dielectric, owner_group, block_slots):
    dma = pltpu.SemaphoreType.DMA
    vmem = pl.BlockSpec(memory_space=pltpu.VMEM)

    def buf(*shape):
        return pltpu.VMEM(shape + (128,), F32)

    return pl.pallas_call(
        kernel,
        out_shape=pltpu.VMEM((2, 1, 10, 40, 128), F32),
        in_specs=[pl.BlockSpec(memory_space=pl.ANY)] * 4,
        out_specs=vmem,
        scratch_shapes=[
            buf(RES, XS, 40), buf(XS, 40), pltpu.SMEM((2,), jnp.int32), pltpu.SMEM((2, 4), jnp.int32),
            dma((PAIRS,)), dma((3,)),
            buf(PAIRS, 4, RES, 24), buf(7, GROUPS, RES, 24), buf(PAIRS, ORBS, 8), buf(7, ORBS, 8),
            buf(2, RES + 1, 24), buf(2, RES + 1, 24), buf(2, PAIRS, 32), buf(7, 32),
            buf(ORBS, ROWS), buf(ORBS, ROWS), buf(ORBS, ROWS),
            buf(ROWS), buf(ROWS), buf(ROWS), buf(ROWS), buf(2, ROWS),
            buf(13, COUP), buf(13, COUP), buf(8, CHUNKS * 8),
            buf(5, GROUPS, 40), buf(5, 4, 40),
            dma((PAIRS, 4)), dma((PAIRS, 4)), dma((PAIRS,)),
            dma((PAIRS,)), dma((PAIRS,)), dma((2,)), dma((2,)), dma((2,)), dma((2,)), dma((2,)), dma((2,)),
            dma, dma, dma, dma((2,)), dma((2,)), dma((5, GROUPS)), dma((5, 4)), dma((5,)),
        ],
        compiler_params=pltpu.CompilerParams(collective_id=0, has_side_effects=True, vmem_limit_bytes=60 << 20),
        cost_estimate=pl.CostEstimate(flops=60_000_000, bytes_accessed=2_500_000, transcendentals=0),
    )(orbitals, dielectric, owner_group, block_slots)


def solution(mesh):
    in_specs = (P("orb", "gx", "gy", None), P("gx", "gy", None), P(), P())
    out_specs = P(None, "orb", "gx", "gy", None)
    return jax.shard_map(shards, mesh=mesh, in_specs=in_specs, out_specs=out_specs, check_vma=False)
```

```python
import math

import jax
import jax.numpy as jnp
from jax import lax
from jax.experimental import pallas as pl
from jax.experimental.pallas import tpu as pltpu
from jax.sharding import PartitionSpec as P

MESH = pl.DeviceIdType.MESH
F32 = jnp.float32

MIXING = 0.25
LOWEST = 0.5
HIGHEST = 24.0
MID = (HIGHEST + LOWEST) / 2.0
HALF = (HIGHEST - LOWEST) / 2.0
RATIO = MID / HALF
R0 = 1.0 / RATIO
R1 = 1.0 / (2.0 * RATIO - R0)
R2 = 1.0 / (2.0 * RATIO - R1)
K1, K2 = R1 * R0, R2 * R1
S1, S2 = 2.0 * R1 / HALF, 2.0 * R2 / HALF
Q = 1.0 / MID
ALPHA, BETA = K1 * Q + S1, S1 * Q
SCALE = -MIXING * 4.0 * math.pi
C0 = SCALE * (Q + ALPHA + K2 * ALPHA + S2)
C1 = -SCALE * (BETA + K2 * BETA + S2 * (Q + ALPHA))
C2 = SCALE * S2 * BETA

GROUPS = 4
RES = 8
ORBS = 32
XS = 10
SUB = 10
ROW = 14
PAIRS = 5
BASE = 18
FIRST = BASE + 2 * ROW + 2
LEAD = 32
ROWS = 240
CHUNKS = 17
LEAD_CHUNKS = 4
COUP = (CHUNKS + LEAD_CHUNKS) * 8
STARTS = (-2, 10, 18, 30)
ORDER = (0, 4, 1, 3, 2)
PIECES = (0, 8, 2, 4, 6)


def kernel(
    orb_in, diel_in, owner_in, slots_in, out,
    orb, diel, owner, slots, s_in, s_small, send, rb, sib_s, sib_r, ys, yr, ds_, db, w, wz, wz2, wd, kx, ky, kz, dd, coup, dens, flat, ob, orr,
    s_send, r_send, l_send, s_sib, r_sib, s_y, r_y, s_x, r_x, s_xs, r_xs, s_d, r_d, l_d, s_dx, r_dx, s_o, r_o, l_o, ready,
):
    g, gx, gy = lax.axis_index("orb"), lax.axis_index("gx"), lax.axis_index("gy")
    zl, c = gy // 2, lax.rem(gy, 2)
    home = g // 2
    mine = c == home
    part = lax.rem(g, 2)
    sibling = (g, gx, 2 * zl + 1 - c)
    left, right = (g, lax.rem(gx + 15, 16), gy), (g, lax.rem(gx + 1, 16), gy)
    down, up = (g, gx, lax.rem(gy + 3, 4)), (g, gx, lax.rem(gy + 1, 4))

    def remote(src, dst, ss, rs, to):
        return pltpu.make_async_remote_copy(
            src_ref=src, dst_ref=dst, send_sem=ss, recv_sem=rs, device_id=to, device_id_type=MESH
        )

    loads = [
        pltpu.make_async_copy(orb_in.at[:, pl.ds(2 * p, 2)], orb.at[:, pl.ds(2 * p, 2)], s_in.at[p]) for p in range(PAIRS)
    ]
    small = [
        pltpu.make_async_copy(a, b, s_small.at[n])
        for n, (a, b) in enumerate(((diel_in, diel), (owner_in, owner), (slots_in, slots)))
    ]
    for p in ORDER:
        loads[p].start()
    for copy in small:
        copy.start()

    barrier = pltpu.get_barrier_semaphore()
    for dg in range(GROUPS):
        for dc in range(2):
            if dg or dc:
                to = (lax.rem(g + dg, GROUPS), gx, 2 * zl + (c if dc == 0 else 1 - c))
                pl.semaphore_signal(barrier, inc=1, device_id=to, device_id_type=MESH)
    across = (g, gx, lax.rem(gy + 3 + 2 * c, 4))
    for to in (left, across):
        pl.semaphore_signal(barrier, inc=1, device_id=to, device_id_type=MESH)

    def pack(p, which):
        def body(f, carry):
            for xx in range(2):
                x = 2 * p + xx
                at = pl.multiple_of(24 * f, 8)
                for wi in which:
                    o = 12 * xx
                    if wi == 0:
                        send[p, wi, f, o : o + 2, :] = yr[0, f, 2 * x : 2 * x + 2, :]
                        send[p, wi, f, o + 2 : o + 12, :] = orb[f, x, 0:10, :]
                    elif wi == 3:
                        send[p, wi, f, o : o + 10, :] = orb[f, x, 30:40, :]
                        send[p, wi, f, o + 10 : o + 12, :] = yr[1, f, 2 * x : 2 * x + 2, :]
                    else:
                        send[p, wi, f, o : o + 12, :] = orb[f, x, STARTS[wi] : STARTS[wi] + 12, :]
            return carry

        lax.fori_loop(0, RES, body, 0)

    def share_copy(p, wi):
        to = (2 * c + wi // 2, gx, 2 * zl + wi % 2)
        here = jnp.logical_and(to[0] == g, c == wi % 2)
        away = remote(send.at[p, wi], rb.at[p + 1, g], s_send.at[p, wi], r_send.at[p, g], to)
        near = pltpu.make_async_copy(send.at[p, wi], rb.at[p + 1, g], l_send.at[p])
        return here, away, near

    def share_start(p, wi):
        here, away, near = share_copy(p, wi)
        pl.when(here)(near.start)
        pl.when(jnp.logical_not(here))(away.start)

    def share_sent(p, wi):
        here, away, near = share_copy(p, wi)
        pl.when(jnp.logical_not(here))(away.wait_send)

    def share_arrived(p, source):
        near_one = jnp.logical_and(g == source, mine)
        near = pltpu.make_async_copy(send.at[p, 0], rb.at[p + 1, source], l_send.at[p])
        away = remote(send.at[p, 0], rb.at[p + 1, source], s_send.at[p, 0], r_send.at[p, source], sibling)
        pl.when(near_one)(near.wait)
        pl.when(jnp.logical_not(near_one))(away.wait_recv)

    loads[0].wait()
    pack(0, (1, 2))
    pl.semaphore_wait(barrier, 9)
    pl.semaphore_signal(ready, inc=1, device_id=right, device_id_type=MESH)
    share_start(0, 1)
    share_start(0, 2)
    for copy in loads[1:] + small:
        copy.wait()

    def pack_ends(f, carry):
        for x in range(XS):
            ys[0, f, 2 * x : 2 * x + 2, :] = orb[f, x, 0:2, :]
            ys[1, f, 2 * x : 2 * x + 2, :] = orb[f, x, 38:40, :]
        return carry

    lax.fori_loop(0, RES, pack_ends, 0)
    for x in range(XS):
        ys[0, RES, 2 * x : 2 * x + 2, :] = diel[x, 0:2, :]
        ys[1, RES, 2 * x : 2 * x + 2, :] = diel[x, 38:40, :]
    to_down = remote(ys.at[0], yr.at[1], s_y.at[0], r_y.at[1], down)
    to_up = remote(ys.at[1], yr.at[0], s_y.at[1], r_y.at[0], up)
    to_down.start()
    to_up.start()

    pack(4, (1, 2))
    share_start(4, 1)
    share_start(4, 2)
    to_down.wait()
    to_up.wait()
    for ch in range(2):
        for ph in range(2):

            @pl.when(jnp.logical_and(mine, jnp.logical_and(c == ch, part == ph)))
            def _():
                for k in range(2):
                    wi = 2 * ph + k
                    for x in range(XS):
                        p, o = x // 2, ROW * (x % 2)
                        if wi == 0:
                            ds_[k, p, o : o + 2, :] = yr[0, RES, 2 * x : 2 * x + 2, :]
                            ds_[k, p, o + 2 : o + 14, :] = diel[x, 0:12, :]
                        elif wi == 3:
                            ds_[k, p, o : o + 12, :] = diel[x, 28:40, :]
                            ds_[k, p, o + 12 : o + 14, :] = yr[1, RES, 2 * x : 2 * x + 2, :]
                        else:
                            ds_[k, p, o : o + 14, :] = diel[x, 10 * wi - 2 : 10 * wi + 12, :]
                near = pltpu.make_async_copy(ds_.at[ch], db.at[pl.ds(1, PAIRS)], l_d)
                away = remote(ds_.at[1 - ch], db.at[pl.ds(1, PAIRS)], s_d, r_d, sibling)
                near.start()
                away.start()

    for p in ORDER[:2]:
        pack(p, (0, 3))
        share_start(p, 0)
        share_start(p, 3)

    pack(1, (0, 1, 2, 3))
    share_start(1, 1)
    share_start(1, 2)
    for p in ORDER[3:]:
        pack(p, (0, 1, 2, 3))

    @pl.when(mine)
    def _():
        pltpu.make_async_copy(ds_.at[0], db.at[pl.ds(1, PAIRS)], l_d).wait()
        remote(ds_.at[0], db.at[pl.ds(1, PAIRS)], s_d, r_d, sibling).wait_send()

    @pl.when(jnp.logical_not(mine))
    def _():
        remote(ds_.at[0], db.at[pl.ds(1, PAIRS)], s_d, r_d, sibling).wait_recv()

    d_left = remote(db.at[1], db.at[6], s_dx.at[0], r_dx.at[0], left)
    d_right = remote(db.at[5], db.at[0], s_dx.at[1], r_dx.at[1], right)
    pl.semaphore_wait(ready, 1)
    d_left.start()
    d_right.start()

    def sib_copy(p):
        return remote(sib_s.at[p], sib_r.at[p + 1], s_sib.at[p], r_sib.at[p], sibling)

    def arrive(p):
        for source in range(GROUPS):
            share_arrived(p, source)
        for ch in range(2):

            @pl.when(c == ch)
            def _():
                def body(o, carry):
                    q, f = o // RES, lax.rem(o, RES)
                    for xx in range(2):
                        a = 12 * xx + (10 if ch == 0 else 0)
                        sib_s[p, o, 2 * xx : 2 * xx + 2, :] = rb[p + 1, q, f, a : a + 2, :]
                    return carry

                lax.fori_loop(0, ORBS, body, 0)

        sib_copy(p).start()

    def edge_copies(p):
        to, slot, n = (left, 6, 0) if p == 0 else (right, 0, 1)
        return (
            remote(rb.at[p + 1], rb.at[slot], s_x.at[n], r_x.at[n], to),
            remote(sib_r.at[p + 1], sib_r.at[slot], s_xs.at[n], r_xs.at[n], to),
        )

    def put(o, r, v, first, count):
        for ref, value in ((w, v), (wz, ahead(v)), (wz2, ahead(v, 2))):
            ref[o, r : r + count, :] = value[first : first + count]

    def unpack_main(slot):
        for ch in range(2):

            @pl.when(c == ch)
            def _():
                def body(o, carry):
                    q, f = o // RES, lax.rem(o, RES)
                    for xx in range(2):
                        r = BASE + 28 * slot + ROW * xx + 2 * ch
                        for n in (0, 4):
                            put(o, r + n, rb[slot, q, f, 12 * xx + n : 12 * xx + n + 8, :], 0, 8)
                    return carry

                lax.fori_loop(0, ORBS, body, 0, unroll=2)

    def unpack_sib(slot):
        for ch in range(2):

            @pl.when(c == ch)
            def _():
                def body(o, carry):
                    v = sib_r[slot, o, :, :]
                    for xx in range(2):
                        put(o, BASE + 28 * slot + ROW * xx + 12 * (1 - ch), v, 2 * xx, 2)
                    return carry

                lax.fori_loop(0, ORBS, body, 0, unroll=4)

    def unpack(slot):
        unpack_main(slot)
        unpack_sib(slot)

    def density(k, carry):
        r = pl.multiple_of(FIRST - LEAD + 8 * k, 8)
        d = pl.multiple_of(8 * k, 8)

        def body(i, acc):
            for n in range(4):
                o = 4 * i + n

                def row(ref, shift=0):
                    return ref[o, pl.ds(r + shift, 8), :]

                a, b, b2 = row(w), row(w, 14), row(w, 28)
                y1, y2, xy = row(w, 1), row(w, 2), row(w, 15)
                az, az2, bz, yz = row(wz), row(wz2), row(wz, 14), row(wz, 1)
                terms = (
                    a * a, a * b, a * y1, a * az, a * b2, a * y2, a * az2,
                    a * xy, b * y1, a * bz, az * b, a * yz, az * y1,
                )
                acc = tuple(s + t for s, t in zip(acc, terms))
            return acc

        acc = lax.fori_loop(0, ORBS // 4, body, (jnp.zeros((8, 128), F32),) * 13)
        for n in range(13):
            dens[n, pl.ds(d, 8), :] = coup[n, pl.ds(d, 8), :] * acc[n]
        return carry

    chosen = [owner[n // 4] * RES + slots[n // 4, n % 4] for n in range(8)]

    def apply(k, carry):
        r = pl.multiple_of(FIRST + 8 * k, 8)
        d = pl.multiple_of(LEAD + 8 * k, 8)

        def m(n, back=0):
            return dens[n, pl.ds(d - back, 8), :]

        level = (
            (0, m(0)), (14, m(1)), (-14, m(1, 14)), (1, m(2)), (-1, m(2, 1)), (28, m(4)), (-28, m(4, 28)),
            (2, m(5)), (-2, m(5, 2)), (15, m(7)), (-15, m(7, 15)), (13, m(8, 1)), (-13, m(8, 14)),
        )
        z1, z2 = m(3), m(6)
        lower = ((0, z1), (14, m(10)), (-14, m(9, 14)), (1, m(12)), (-1, m(11, 1)))
        upper = ((0, z1), (14, m(9)), (-14, m(10, 14)), (1, m(11)), (-1, m(12, 1)))
        for n in range(8):
            o = chosen[n]
            v = {s: w[o, pl.ds(r + s, 8), :] for s, _ in level}

            def total(terms):
                while len(terms) > 1:
                    terms = [sum(terms[i + 1 : i + 2], terms[i]) for i in range(0, len(terms), 2)]
                return terms[0]

            below = total([x * v[s] for s, x in lower])
            res = total(
                [x * v[s] for s, x in level]
                + [x * wz[o, pl.ds(r + s, 8), :] for s, x in upper]
                + [z2 * wz2[o, pl.ds(r, 8), :]]
            )
            res = res + pltpu.roll(below, 1, 1) + pltpu.roll(z2 * v[0], 2, 1)
            flat[n, pl.ds(pl.multiple_of(8 * k, 8), 8), :] = res
        return carry

    def out_copy(piece, j):
        to = (j, gx, 2 * zl + home)
        here = jnp.logical_and(g == j, mine)
        slot = 2 * part + c
        source, target = ob.at[piece], orr.at[piece]
        away = remote(source.at[j], target.at[slot], s_o.at[piece, j], r_o.at[piece, slot], to)
        near = pltpu.make_async_copy(source.at[j], target.at[slot], l_o.at[piece])
        return here, away, near

    def out_start(piece):
        first = PIECES[piece]

        def pack_out(j, carry):
            for window in range(2):
                for n in range(2):
                    o, x = 10 * (2 * window + n), first + n
                    ob[piece, j, o : o + 10, :] = flat[4 * window + j, ROW * x : ROW * x + 10, :]
            return carry

        lax.fori_loop(0, GROUPS, pack_out, 0)
        for j in range(GROUPS):
            here, away, near = out_copy(piece, j)
            pl.when(here)(near.start)
            pl.when(jnp.logical_not(here))(away.start)

    def out_place(piece):
        first = PIECES[piece]
        source, target = ob.at[piece], orr.at[piece]
        for wi in range(4):
            here = jnp.logical_and(2 * c + wi // 2 == g, c == wi % 2)
            away = remote(source.at[0], target.at[wi], s_o.at[piece, 0], r_o.at[piece, wi], sibling)
            near = pltpu.make_async_copy(source.at[0], target.at[wi], l_o.at[piece])
            pl.when(here)(near.wait)
            pl.when(jnp.logical_not(here))(away.wait_recv)
            for window in range(2):
                for n in range(2):
                    o = 10 * (2 * window + n)
                    out[window, 0, first + n, 10 * wi : 10 * wi + 10, :] = target[wi, o : o + 10, :]

    arrive(0)
    edge_copies(0)[0].start()
    for wi in range(4):
        share_sent(0, wi)
    for p, wi in ((1, 0), (1, 3), (3, 1), (3, 2)):
        share_start(p, wi)
    arrive(4)
    edge_copies(4)[0].start()
    for wi in range(4):
        share_sent(4, wi)
    for p, wi in ((3, 0), (3, 3)):
        share_start(p, wi)

    d_left.wait()
    d_right.wait()
    wd[...] = jnp.zeros_like(wd)
    for s in range(7):
        wd[BASE + 28 * s : BASE + 28 * s + 28, :] = db[s, 0:28, :]

    lane = lax.broadcasted_iota(jnp.int32, (8, 128), 1)
    top, bottom = lane == 127, lane == 0

    def ahead(v, n=1):
        return pltpu.roll(v, 128 - n, 1)

    def at(ref, r, n=0):
        return ref[r + n : r + n + 8, :]

    for i in range(29):
        r = 8 * i
        if r + 14 + 8 > ROWS:
            break
        e, ex, ey = at(wd, r), at(wd, r, 14), at(wd, r, 1)
        kx[r : r + 8, :] = 0.5 * (e + ex)
        ky[r : r + 8, :] = 0.5 * (e + ey)
        kz[r : r + 8, :] = jnp.where(top, 0.0, 0.5 * (e + ahead(e)))

    def squared(r):
        e = at(wd, r)
        x1, x0, y1, y0 = at(kx, r), at(kx, r, -14), at(ky, r), at(ky, r, -1)
        z1 = at(kz, r)
        z0 = pltpu.roll(z1, 1, 1)
        ends = jnp.where(jnp.logical_or(top, bottom), e, 0.0)
        total = x1 + x0 + y1 + y0 + z1 + z0 + ends
        squares = x1 * x1 + x0 * x0 + y1 * y1 + y0 * y0 + z1 * z1 + z0 * z0
        return total, squares

    for i in range(2, 27):
        r = 8 * i
        total, squares = squared(r)
        dd[0, r : r + 8, :] = total
        dd[1, r : r + 8, :] = squares

    def couplings(k):
        r = FIRST + 8 * k
        d0, sq = at(dd.at[0], r), at(dd.at[1], r)
        x1, y1, z1 = at(kx, r), at(ky, r), at(kz, r)
        dx, dy = at(dd.at[0], r, 14), at(dd.at[0], r, 1)
        xx, yx, zx = at(kx, r, 14), at(ky, r, 14), at(kz, r, 14)
        xy, yy, zy = at(kx, r, 1), at(ky, r, 1), at(kz, r, 1)
        dz, xz, yz, zz = ahead(d0), ahead(x1), ahead(y1), ahead(z1)
        values = (
            C0 + C1 * d0 + C2 * (d0 * d0 + sq),
            -x1 * (C1 + C2 * (d0 + dx)),
            -y1 * (C1 + C2 * (d0 + dy)),
            -z1 * (C1 + C2 * (d0 + dz)),
            C2 * (x1 * xx),
            C2 * (y1 * yy),
            C2 * (z1 * zz),
            C2 * (x1 * yx + y1 * xy),
            C2 * (x1 * y1 + xy * yx),
            C2 * (x1 * zx + z1 * xz),
            C2 * (x1 * z1 + xz * zx),
            C2 * (y1 * zy + z1 * yz),
            C2 * (y1 * z1 + yz * zy),
        )
        for n, v in enumerate(values):
            coup[n, LEAD + 8 * k : LEAD + 8 * k + 8, :] = v

    for k in range(-LEAD_CHUNKS, CHUNKS):
        couplings(k)

    for p in (0, 4):
        sib_copy(p).wait()
        edge_copies(p)[1].start()
        unpack(p + 1)
    arrive(1)
    for wi in range(4):
        share_sent(1, wi)
    for wi in range(4):
        share_start(2, wi)
    unpack_main(2)
    sib_copy(1).wait()
    unpack_sib(2)
    arrive(3)
    unpack_main(4)
    sib_copy(3).wait()
    unpack_sib(4)
    for p in (0, 4):
        for e in edge_copies(p):
            e.wait()
    unpack(0)
    unpack(6)
    lax.fori_loop(0, 7, density, 0)
    lax.fori_loop(0, 3, apply, 0)
    lax.fori_loop(14, 21, density, 0)
    lax.fori_loop(14, 17, apply, 0)
    for p in (3, 2):
        for wi in range(4):
            share_sent(p, wi)
    out_start(0)
    out_start(1)
    arrive(2)
    unpack_main(3)
    sib_copy(2).wait()
    unpack_sib(3)
    lax.fori_loop(7, 11, density, 0)
    lax.fori_loop(3, 7, apply, 0)
    out_start(2)
    lax.fori_loop(11, 14, density, 0)
    lax.fori_loop(7, 10, apply, 0)
    out_start(3)
    lax.fori_loop(14, 15, density, 0)
    lax.fori_loop(10, 14, apply, 0)
    out_start(4)
    for piece in range(len(PIECES)):
        out_place(piece)

    for piece in range(len(PIECES)):
        for j in range(GROUPS):
            here, away, near = out_copy(piece, j)
            pl.when(jnp.logical_not(here))(away.wait_send)


def shards(orbitals, dielectric, owner_group, block_slots):
    dma = pltpu.SemaphoreType.DMA
    vmem = pl.BlockSpec(memory_space=pltpu.VMEM)

    def buf(*shape):
        return pltpu.VMEM(shape + (128,), F32)

    return pl.pallas_call(
        kernel,
        out_shape=pltpu.VMEM((2, 1, 10, 40, 128), F32),
        in_specs=[pl.BlockSpec(memory_space=pl.ANY)] * 4,
        out_specs=vmem,
        scratch_shapes=[
            buf(RES, XS, 40), buf(XS, 40), pltpu.SMEM((2,), jnp.int32), pltpu.SMEM((2, 4), jnp.int32),
            dma((PAIRS,)), dma((3,)),
            buf(PAIRS, 4, RES, 24), buf(7, GROUPS, RES, 24), buf(PAIRS, ORBS, 8), buf(7, ORBS, 8),
            buf(2, RES + 1, 24), buf(2, RES + 1, 24), buf(2, PAIRS, 32), buf(7, 32),
            buf(ORBS, ROWS), buf(ORBS, ROWS), buf(ORBS, ROWS),
            buf(ROWS), buf(ROWS), buf(ROWS), buf(ROWS), buf(2, ROWS),
            buf(13, COUP), buf(13, COUP), buf(8, CHUNKS * 8),
            buf(5, GROUPS, 40), buf(5, 4, 40),
            dma((PAIRS, 4)), dma((PAIRS, 4)), dma((PAIRS,)),
            dma((PAIRS,)), dma((PAIRS,)), dma((2,)), dma((2,)), dma((2,)), dma((2,)), dma((2,)), dma((2,)),
            dma, dma, dma, dma((2,)), dma((2,)), dma((5, GROUPS)), dma((5, 4)), dma((5,)), pltpu.SemaphoreType.REGULAR,
        ],
        compiler_params=pltpu.CompilerParams(collective_id=0, has_side_effects=True, vmem_limit_bytes=60 << 20),
        cost_estimate=pl.CostEstimate(flops=60_000_000, bytes_accessed=2_500_000, transcendentals=0),
    )(orbitals, dielectric, owner_group, block_slots)


def solution(mesh):
    in_specs = (P("orb", "gx", "gy", None), P("gx", "gy", None), P(), P())
    out_specs = P(None, "orb", "gx", "gy", None)
    return jax.shard_map(shards, mesh=mesh, in_specs=in_specs, out_specs=out_specs, check_vma=False)
```

```python
import math

import jax
import jax.numpy as jnp
from jax import lax
from jax.experimental import pallas as pl
from jax.experimental.pallas import tpu as pltpu
from jax.sharding import PartitionSpec as P

MESH = pl.DeviceIdType.MESH
F32 = jnp.float32

MIXING = 0.25
LOWEST = 0.5
HIGHEST = 24.0
MID = (HIGHEST + LOWEST) / 2.0
HALF = (HIGHEST - LOWEST) / 2.0
RATIO = MID / HALF
R0 = 1.0 / RATIO
R1 = 1.0 / (2.0 * RATIO - R0)
R2 = 1.0 / (2.0 * RATIO - R1)
K1, K2 = R1 * R0, R2 * R1
S1, S2 = 2.0 * R1 / HALF, 2.0 * R2 / HALF
Q = 1.0 / MID
ALPHA, BETA = K1 * Q + S1, S1 * Q
SCALE = -MIXING * 4.0 * math.pi
C0 = SCALE * (Q + ALPHA + K2 * ALPHA + S2)
C1 = -SCALE * (BETA + K2 * BETA + S2 * (Q + ALPHA))
C2 = SCALE * S2 * BETA

GROUPS = 4
RES = 8
ORBS = 32
XS = 10
SUB = 10
ROW = 14
PAIRS = 5
BASE = 18
FIRST = BASE + 2 * ROW + 2
LEAD = 32
ROWS = 240
CHUNKS = 17
LEAD_CHUNKS = 4
COUP = (CHUNKS + LEAD_CHUNKS) * 8
STARTS = (-2, 10, 18, 30)
ORDER = (0, 4, 1, 3, 2)
PIECES = (0, 8, 2, 4, 6)


def kernel(
    orb_in, diel_in, owner_in, slots_in, out,
    orb, diel, owner, slots, s_in, s_small, send, rb, sib_s, sib_r, ys, yr, ds_, db, w, wz, wz2, wd, kx, ky, kz, dd, coup, dens, flat, ob, orr,
    s_send, r_send, l_send, s_sib, r_sib, s_y, r_y, s_x, r_x, s_xs, r_xs, s_d, r_d, l_d, s_dx, r_dx, s_o, r_o, l_o, ready,
):
    g, gx, gy = lax.axis_index("orb"), lax.axis_index("gx"), lax.axis_index("gy")
    zl, c = gy // 2, lax.rem(gy, 2)
    home = g // 2
    mine = c == home
    part = lax.rem(g, 2)
    sibling = (g, gx, 2 * zl + 1 - c)
    left, right = (g, lax.rem(gx + 15, 16), gy), (g, lax.rem(gx + 1, 16), gy)
    down, up = (g, gx, lax.rem(gy + 3, 4)), (g, gx, lax.rem(gy + 1, 4))

    def remote(src, dst, ss, rs, to):
        return pltpu.make_async_remote_copy(
            src_ref=src, dst_ref=dst, send_sem=ss, recv_sem=rs, device_id=to, device_id_type=MESH
        )

    loads = [
        pltpu.make_async_copy(orb_in.at[:, pl.ds(2 * p, 2)], orb.at[:, pl.ds(2 * p, 2)], s_in.at[p]) for p in range(PAIRS)
    ]
    small = [
        pltpu.make_async_copy(a, b, s_small.at[n])
        for n, (a, b) in enumerate(((diel_in, diel), (owner_in, owner), (slots_in, slots)))
    ]
    for p in ORDER:
        loads[p].start()
    for copy in small:
        copy.start()

    barrier = pltpu.get_barrier_semaphore()
    for dg in range(GROUPS):
        for dc in range(2):
            if dg or dc:
                to = (lax.rem(g + dg, GROUPS), gx, 2 * zl + (c if dc == 0 else 1 - c))
                pl.semaphore_signal(barrier, inc=1, device_id=to, device_id_type=MESH)
    across = (g, gx, lax.rem(gy + 3 + 2 * c, 4))
    for to in (left, across):
        pl.semaphore_signal(barrier, inc=1, device_id=to, device_id_type=MESH)

    def pack(p, which):
        def body(f, carry):
            for xx in range(2):
                x = 2 * p + xx
                at = pl.multiple_of(24 * f, 8)
                for wi in which:
                    o = 12 * xx
                    if wi == 0:
                        send[p, wi, f, o : o + 2, :] = yr[0, f, 2 * x : 2 * x + 2, :]
                        send[p, wi, f, o + 2 : o + 12, :] = orb[f, x, 0:10, :]
                    elif wi == 3:
                        send[p, wi, f, o : o + 10, :] = orb[f, x, 30:40, :]
                        send[p, wi, f, o + 10 : o + 12, :] = yr[1, f, 2 * x : 2 * x + 2, :]
                    else:
                        send[p, wi, f, o : o + 12, :] = orb[f, x, STARTS[wi] : STARTS[wi] + 12, :]
            return carry

        lax.fori_loop(0, RES, body, 0)

    def share_copy(p, wi):
        to = (2 * c + wi // 2, gx, 2 * zl + wi % 2)
        here = jnp.logical_and(to[0] == g, c == wi % 2)
        away = remote(send.at[p, wi], rb.at[p + 1, g], s_send.at[p, wi], r_send.at[p, g], to)
        near = pltpu.make_async_copy(send.at[p, wi], rb.at[p + 1, g], l_send.at[p])
        return here, away, near

    def share_start(p, wi):
        here, away, near = share_copy(p, wi)
        pl.when(here)(near.start)
        pl.when(jnp.logical_not(here))(away.start)

    def share_sent(p, wi):
        here, away, near = share_copy(p, wi)
        pl.when(jnp.logical_not(here))(away.wait_send)

    def share_arrived(p, source):
        near_one = jnp.logical_and(g == source, mine)
        near = pltpu.make_async_copy(send.at[p, 0], rb.at[p + 1, source], l_send.at[p])
        away = remote(send.at[p, 0], rb.at[p + 1, source], s_send.at[p, 0], r_send.at[p, source], sibling)
        pl.when(near_one)(near.wait)
        pl.when(jnp.logical_not(near_one))(away.wait_recv)

    loads[0].wait()
    pack(0, (1, 2))
    pl.semaphore_wait(barrier, 9)
    pl.semaphore_signal(ready, inc=1, device_id=right, device_id_type=MESH)
    share_start(0, 1)
    share_start(0, 2)
    for copy in loads[1:] + small:
        copy.wait()

    def pack_ends(f, carry):
        for x in range(XS):
            ys[0, f, 2 * x : 2 * x + 2, :] = orb[f, x, 0:2, :]
            ys[1, f, 2 * x : 2 * x + 2, :] = orb[f, x, 38:40, :]
        return carry

    lax.fori_loop(0, RES, pack_ends, 0)
    for x in range(XS):
        ys[0, RES, 2 * x : 2 * x + 2, :] = diel[x, 0:2, :]
        ys[1, RES, 2 * x : 2 * x + 2, :] = diel[x, 38:40, :]
    to_down = remote(ys.at[0], yr.at[1], s_y.at[0], r_y.at[1], down)
    to_up = remote(ys.at[1], yr.at[0], s_y.at[1], r_y.at[0], up)
    to_down.start()
    to_up.start()

    pack(4, (1, 2))
    share_start(4, 1)
    share_start(4, 2)
    to_down.wait()
    to_up.wait()
    for ch in range(2):
        for ph in range(2):

            @pl.when(jnp.logical_and(mine, jnp.logical_and(c == ch, part == ph)))
            def _():
                for k in range(2):
                    wi = 2 * ph + k
                    for x in range(XS):
                        p, o = x // 2, ROW * (x % 2)
                        if wi == 0:
                            ds_[k, p, o : o + 2, :] = yr[0, RES, 2 * x : 2 * x + 2, :]
                            ds_[k, p, o + 2 : o + 14, :] = diel[x, 0:12, :]
                        elif wi == 3:
                            ds_[k, p, o : o + 12, :] = diel[x, 28:40, :]
                            ds_[k, p, o + 12 : o + 14, :] = yr[1, RES, 2 * x : 2 * x + 2, :]
                        else:
                            ds_[k, p, o : o + 14, :] = diel[x, 10 * wi - 2 : 10 * wi + 12, :]
                near = pltpu.make_async_copy(ds_.at[ch], db.at[pl.ds(1, PAIRS)], l_d)
                away = remote(ds_.at[1 - ch], db.at[pl.ds(1, PAIRS)], s_d, r_d, sibling)
                near.start()
                away.start()

    for p in ORDER[:2]:
        pack(p, (0, 3))
        share_start(p, 0)
        share_start(p, 3)

    pack(1, (0, 1, 2, 3))
    share_start(1, 1)
    share_start(1, 2)
    for p in ORDER[3:]:
        pack(p, (0, 1, 2, 3))

    @pl.when(mine)
    def _():
        pltpu.make_async_copy(ds_.at[0], db.at[pl.ds(1, PAIRS)], l_d).wait()
        remote(ds_.at[0], db.at[pl.ds(1, PAIRS)], s_d, r_d, sibling).wait_send()

    @pl.when(jnp.logical_not(mine))
    def _():
        remote(ds_.at[0], db.at[pl.ds(1, PAIRS)], s_d, r_d, sibling).wait_recv()

    d_left = remote(db.at[1], db.at[6], s_dx.at[0], r_dx.at[0], left)
    d_right = remote(db.at[5], db.at[0], s_dx.at[1], r_dx.at[1], right)
    pl.semaphore_wait(ready, 1)
    d_left.start()
    d_right.start()

    def sib_copy(p):
        return remote(sib_s.at[p], sib_r.at[p + 1], s_sib.at[p], r_sib.at[p], sibling)

    def arrive(p):
        for source in range(GROUPS):
            share_arrived(p, source)
        for ch in range(2):

            @pl.when(c == ch)
            def _():
                def body(o, carry):
                    q, f = o // RES, lax.rem(o, RES)
                    for xx in range(2):
                        a = 12 * xx + (10 if ch == 0 else 0)
                        sib_s[p, o, 2 * xx : 2 * xx + 2, :] = rb[p + 1, q, f, a : a + 2, :]
                    return carry

                lax.fori_loop(0, ORBS, body, 0, unroll=4)

        sib_copy(p).start()

    def edge_copies(p):
        to, slot, n = (left, 6, 0) if p == 0 else (right, 0, 1)
        return (
            remote(rb.at[p + 1], rb.at[slot], s_x.at[n], r_x.at[n], to),
            remote(sib_r.at[p + 1], sib_r.at[slot], s_xs.at[n], r_xs.at[n], to),
        )

    def put(o, r, v, first, count):
        for ref, value in ((w, v), (wz, ahead(v)), (wz2, ahead(v, 2))):
            ref[o, r : r + count, :] = value[first : first + count]

    def unpack_main(slot):
        for ch in range(2):

            @pl.when(c == ch)
            def _():
                def body(o, carry):
                    q, f = o // RES, lax.rem(o, RES)
                    for xx in range(2):
                        r = BASE + 28 * slot + ROW * xx + 2 * ch
                        for n in (0, 4):
                            put(o, r + n, rb[slot, q, f, 12 * xx + n : 12 * xx + n + 8, :], 0, 8)
                    return carry

                lax.fori_loop(0, ORBS, body, 0, unroll=8)

    def unpack_sib(slot):
        for ch in range(2):

            @pl.when(c == ch)
            def _():
                def body(o, carry):
                    v = sib_r[slot, o, :, :]
                    for xx in range(2):
                        put(o, BASE + 28 * slot + ROW * xx + 12 * (1 - ch), v, 2 * xx, 2)
                    return carry

                lax.fori_loop(0, ORBS, body, 0, unroll=16)

    def unpack(slot):
        unpack_main(slot)
        unpack_sib(slot)

    def density(k, carry):
        r = pl.multiple_of(FIRST - LEAD + 8 * k, 8)
        d = pl.multiple_of(8 * k, 8)

        def body(i, acc):
            for n in range(4):
                o = 4 * i + n

                def row(ref, shift=0):
                    return ref[o, pl.ds(r + shift, 8), :]

                a, b, b2 = row(w), row(w, 14), row(w, 28)
                y1, y2, xy = row(w, 1), row(w, 2), row(w, 15)
                az, az2, bz, yz = row(wz), row(wz2), row(wz, 14), row(wz, 1)
                terms = (
                    a * a, a * b, a * y1, a * az, a * b2, a * y2, a * az2,
                    a * xy, b * y1, a * bz, az * b, a * yz, az * y1,
                )
                acc = tuple(s + t for s, t in zip(acc, terms))
            return acc

        acc = lax.fori_loop(0, ORBS // 4, body, (jnp.zeros((8, 128), F32),) * 13)
        for n in range(13):
            dens[n, pl.ds(d, 8), :] = coup[n, pl.ds(d, 8), :] * acc[n]
        return carry

    chosen = [owner[n // 4] * RES + slots[n // 4, n % 4] for n in range(8)]

    def apply(k, carry):
        r = pl.multiple_of(FIRST + 8 * k, 8)
        d = pl.multiple_of(LEAD + 8 * k, 8)

        def m(n, back=0):
            return dens[n, pl.ds(d - back, 8), :]

        level = (
            (0, m(0)), (14, m(1)), (-14, m(1, 14)), (1, m(2)), (-1, m(2, 1)), (28, m(4)), (-28, m(4, 28)),
            (2, m(5)), (-2, m(5, 2)), (15, m(7)), (-15, m(7, 15)), (13, m(8, 1)), (-13, m(8, 14)),
        )
        z1, z2 = m(3), m(6)
        lower = ((0, z1), (14, m(10)), (-14, m(9, 14)), (1, m(12)), (-1, m(11, 1)))
        upper = ((0, z1), (14, m(9)), (-14, m(10, 14)), (1, m(11)), (-1, m(12, 1)))
        for n in range(8):
            o = chosen[n]
            v = {s: w[o, pl.ds(r + s, 8), :] for s, _ in level}

            def total(terms):
                while len(terms) > 1:
                    terms = [sum(terms[i + 1 : i + 2], terms[i]) for i in range(0, len(terms), 2)]
                return terms[0]

            below = total([x * v[s] for s, x in lower])
            res = total(
                [x * v[s] for s, x in level]
                + [x * wz[o, pl.ds(r + s, 8), :] for s, x in upper]
                + [z2 * wz2[o, pl.ds(r, 8), :]]
            )
            res = res + pltpu.roll(below, 1, 1) + pltpu.roll(z2 * v[0], 2, 1)
            flat[n, pl.ds(pl.multiple_of(8 * k, 8), 8), :] = res
        return carry

    def out_copy(piece, j):
        to = (j, gx, 2 * zl + home)
        here = jnp.logical_and(g == j, mine)
        slot = 2 * part + c
        source, target = ob.at[piece], orr.at[piece]
        away = remote(source.at[j], target.at[slot], s_o.at[piece, j], r_o.at[piece, slot], to)
        near = pltpu.make_async_copy(source.at[j], target.at[slot], l_o.at[piece])
        return here, away, near

    def out_start(piece):
        first = PIECES[piece]

        def pack_out(j, carry):
            for window in range(2):
                for n in range(2):
                    o, x = 10 * (2 * window + n), first + n
                    ob[piece, j, o : o + 10, :] = flat[4 * window + j, ROW * x : ROW * x + 10, :]
            return carry

        lax.fori_loop(0, GROUPS, pack_out, 0)
        for j in range(GROUPS):
            here, away, near = out_copy(piece, j)
            pl.when(here)(near.start)
            pl.when(jnp.logical_not(here))(away.start)

    def out_place(piece):
        first = PIECES[piece]
        source, target = ob.at[piece], orr.at[piece]
        for wi in range(4):
            here = jnp.logical_and(2 * c + wi // 2 == g, c == wi % 2)
            away = remote(source.at[0], target.at[wi], s_o.at[piece, 0], r_o.at[piece, wi], sibling)
            near = pltpu.make_async_copy(source.at[0], target.at[wi], l_o.at[piece])
            pl.when(here)(near.wait)
            pl.when(jnp.logical_not(here))(away.wait_recv)
            for window in range(2):
                for n in range(2):
                    o = 10 * (2 * window + n)
                    out[window, 0, first + n, 10 * wi : 10 * wi + 10, :] = target[wi, o : o + 10, :]

    arrive(0)
    edge_copies(0)[0].start()
    for wi in range(4):
        share_sent(0, wi)
    share_start(1, 0)
    share_start(1, 3)
    arrive(4)
    edge_copies(4)[0].start()
    for wi in range(4):
        share_sent(4, wi)
    share_start(3, 1)
    share_start(3, 2)
    share_start(3, 0)
    share_start(3, 3)

    d_left.wait()
    d_right.wait()
    wd[...] = jnp.zeros_like(wd)
    for s in range(7):
        wd[BASE + 28 * s : BASE + 28 * s + 28, :] = db[s, 0:28, :]

    lane = lax.broadcasted_iota(jnp.int32, (8, 128), 1)
    top, bottom = lane == 127, lane == 0

    def ahead(v, n=1):
        return pltpu.roll(v, 128 - n, 1)

    def at(ref, r, n=0):
        return ref[r + n : r + n + 8, :]

    for i in range(29):
        r = 8 * i
        if r + 14 + 8 > ROWS:
            break
        e, ex, ey = at(wd, r), at(wd, r, 14), at(wd, r, 1)
        kx[r : r + 8, :] = 0.5 * (e + ex)
        ky[r : r + 8, :] = 0.5 * (e + ey)
        kz[r : r + 8, :] = jnp.where(top, 0.0, 0.5 * (e + ahead(e)))

    def squared(r):
        e = at(wd, r)
        x1, x0, y1, y0 = at(kx, r), at(kx, r, -14), at(ky, r), at(ky, r, -1)
        z1 = at(kz, r)
        z0 = pltpu.roll(z1, 1, 1)
        ends = jnp.where(jnp.logical_or(top, bottom), e, 0.0)
        total = x1 + x0 + y1 + y0 + z1 + z0 + ends
        squares = x1 * x1 + x0 * x0 + y1 * y1 + y0 * y0 + z1 * z1 + z0 * z0
        return total, squares

    for i in range(2, 27):
        r = 8 * i
        total, squares = squared(r)
        dd[0, r : r + 8, :] = total
        dd[1, r : r + 8, :] = squares

    def couplings(k):
        r = FIRST + 8 * k
        d0, sq = at(dd.at[0], r), at(dd.at[1], r)
        x1, y1, z1 = at(kx, r), at(ky, r), at(kz, r)
        dx, dy = at(dd.at[0], r, 14), at(dd.at[0], r, 1)
        xx, yx, zx = at(kx, r, 14), at(ky, r, 14), at(kz, r, 14)
        xy, yy, zy = at(kx, r, 1), at(ky, r, 1), at(kz, r, 1)
        dz, xz, yz, zz = ahead(d0), ahead(x1), ahead(y1), ahead(z1)
        values = (
            C0 + C1 * d0 + C2 * (d0 * d0 + sq),
            -x1 * (C1 + C2 * (d0 + dx)),
            -y1 * (C1 + C2 * (d0 + dy)),
            -z1 * (C1 + C2 * (d0 + dz)),
            C2 * (x1 * xx),
            C2 * (y1 * yy),
            C2 * (z1 * zz),
            C2 * (x1 * yx + y1 * xy),
            C2 * (x1 * y1 + xy * yx),
            C2 * (x1 * zx + z1 * xz),
            C2 * (x1 * z1 + xz * zx),
            C2 * (y1 * zy + z1 * yz),
            C2 * (y1 * z1 + yz * zy),
        )
        for n, v in enumerate(values):
            coup[n, LEAD + 8 * k : LEAD + 8 * k + 8, :] = v

    for k in range(-LEAD_CHUNKS, CHUNKS):
        couplings(k)

    for p in (0, 4):
        sib_copy(p).wait()
        edge_copies(p)[1].start()
        unpack(p + 1)
    arrive(1)
    for wi in range(4):
        share_sent(1, wi)
    share_start(2, 1)
    share_start(2, 2)
    unpack_main(2)
    sib_copy(1).wait()
    unpack_sib(2)
    share_sent(3, 1)
    share_sent(3, 2)
    share_start(2, 0)
    share_start(2, 3)
    arrive(3)
    unpack_main(4)
    sib_copy(3).wait()
    unpack_sib(4)
    for p in (0, 4):
        for e in edge_copies(p):
            e.wait()
    unpack(0)
    unpack(6)
    lax.fori_loop(0, 7, density, 0)
    lax.fori_loop(0, 3, apply, 0)
    lax.fori_loop(14, 21, density, 0)
    lax.fori_loop(14, 17, apply, 0)
    share_sent(3, 0)
    share_sent(3, 3)
    share_sent(2, 1)
    share_sent(2, 2)
    share_sent(2, 0)
    share_sent(2, 3)
    out_start(0)
    out_start(1)
    arrive(2)
    unpack_main(3)
    sib_copy(2).wait()
    unpack_sib(3)
    lax.fori_loop(7, 11, density, 0)
    lax.fori_loop(3, 7, apply, 0)
    out_start(2)
    lax.fori_loop(11, 14, density, 0)
    lax.fori_loop(7, 10, apply, 0)
    out_start(3)
    lax.fori_loop(14, 15, density, 0)
    lax.fori_loop(10, 14, apply, 0)
    out_start(4)
    for piece in range(len(PIECES)):
        out_place(piece)

    for piece in range(len(PIECES)):
        for j in range(GROUPS):
            here, away, near = out_copy(piece, j)
            pl.when(jnp.logical_not(here))(away.wait_send)


def shards(orbitals, dielectric, owner_group, block_slots):
    dma = pltpu.SemaphoreType.DMA
    vmem = pl.BlockSpec(memory_space=pltpu.VMEM)

    def buf(*shape):
        return pltpu.VMEM(shape + (128,), F32)

    return pl.pallas_call(
        kernel,
        out_shape=pltpu.VMEM((2, 1, 10, 40, 128), F32),
        in_specs=[pl.BlockSpec(memory_space=pl.ANY)] * 4,
        out_specs=vmem,
        scratch_shapes=[
            buf(RES, XS, 40), buf(XS, 40), pltpu.SMEM((2,), jnp.int32), pltpu.SMEM((2, 4), jnp.int32),
            dma((PAIRS,)), dma((3,)),
            buf(PAIRS, 4, RES, 24), buf(7, GROUPS, RES, 24), buf(PAIRS, ORBS, 8), buf(7, ORBS, 8),
            buf(2, RES + 1, 24), buf(2, RES + 1, 24), buf(2, PAIRS, 32), buf(7, 32),
            buf(ORBS, ROWS), buf(ORBS, ROWS), buf(ORBS, ROWS),
            buf(ROWS), buf(ROWS), buf(ROWS), buf(ROWS), buf(2, ROWS),
            buf(13, COUP), buf(13, COUP), buf(8, CHUNKS * 8),
            buf(5, GROUPS, 40), buf(5, 4, 40),
            dma((PAIRS, 4)), dma((PAIRS, 4)), dma((PAIRS,)),
            dma((PAIRS,)), dma((PAIRS,)), dma((2,)), dma((2,)), dma((2,)), dma((2,)), dma((2,)), dma((2,)),
            dma, dma, dma, dma((2,)), dma((2,)), dma((5, GROUPS)), dma((5, 4)), dma((5,)), pltpu.SemaphoreType.REGULAR,
        ],
        compiler_params=pltpu.CompilerParams(collective_id=0, has_side_effects=True, vmem_limit_bytes=60 << 20),
        cost_estimate=pl.CostEstimate(flops=60_000_000, bytes_accessed=2_500_000, transcendentals=0),
    )(orbitals, dielectric, owner_group, block_slots)


def solution(mesh):
    in_specs = (P("orb", "gx", "gy", None), P("gx", "gy", None), P(), P())
    out_specs = P(None, "orb", "gx", "gy", None)
    return jax.shard_map(shards, mesh=mesh, in_specs=in_specs, out_specs=out_specs, check_vma=False)
```

```python
import math

import jax
import jax.numpy as jnp
from jax import lax
from jax.experimental import pallas as pl
from jax.experimental.pallas import tpu as pltpu
from jax.sharding import PartitionSpec as P

MESH = pl.DeviceIdType.MESH
F32 = jnp.float32

MIXING = 0.25
LOWEST = 0.5
HIGHEST = 24.0
MID = (HIGHEST + LOWEST) / 2.0
HALF = (HIGHEST - LOWEST) / 2.0
RATIO = MID / HALF
R0 = 1.0 / RATIO
R1 = 1.0 / (2.0 * RATIO - R0)
R2 = 1.0 / (2.0 * RATIO - R1)
K1, K2 = R1 * R0, R2 * R1
S1, S2 = 2.0 * R1 / HALF, 2.0 * R2 / HALF
Q = 1.0 / MID
ALPHA, BETA = K1 * Q + S1, S1 * Q
SCALE = -MIXING * 4.0 * math.pi
C0 = SCALE * (Q + ALPHA + K2 * ALPHA + S2)
C1 = -SCALE * (BETA + K2 * BETA + S2 * (Q + ALPHA))
C2 = SCALE * S2 * BETA

GROUPS = 4
RES = 8
ORBS = 32
XS = 10
SUB = 10
ROW = 14
PAIRS = 5
BASE = 18
FIRST = BASE + 2 * ROW + 2
LEAD = 32
ROWS = 240
CHUNKS = 17
LEAD_CHUNKS = 4
COUP = (CHUNKS + LEAD_CHUNKS) * 8
STARTS = (-2, 10, 18, 30)
ORDER = (0, 4, 1, 3, 2)
PIECES = (0, 8, 2, 4, 6)


def kernel(
    orb_in, diel_in, owner_in, slots_in, out,
    orb, diel, owner, slots, s_in, s_small, send, rb, sib_s, sib_r, ys, yr, ds_, db, w, wz, wz2, wd, kx, ky, kz, dd, coup, dens, flat, ob, orr,
    s_send, r_send, l_send, s_sib, r_sib, s_y, r_y, s_x, r_x, s_xs, r_xs, s_d, r_d, l_d, s_dx, r_dx, s_o, r_o, l_o, ready,
):
    g, gx, gy = lax.axis_index("orb"), lax.axis_index("gx"), lax.axis_index("gy")
    zl, c = gy // 2, lax.rem(gy, 2)
    home = g // 2
    mine = c == home
    part = lax.rem(g, 2)
    sibling = (g, gx, 2 * zl + 1 - c)
    left, right = (g, lax.rem(gx + 15, 16), gy), (g, lax.rem(gx + 1, 16), gy)
    down, up = (g, gx, lax.rem(gy + 3, 4)), (g, gx, lax.rem(gy + 1, 4))

    def remote(src, dst, ss, rs, to):
        return pltpu.make_async_remote_copy(
            src_ref=src, dst_ref=dst, send_sem=ss, recv_sem=rs, device_id=to, device_id_type=MESH
        )

    loads = [
        pltpu.make_async_copy(orb_in.at[:, pl.ds(2 * p, 2)], orb.at[:, pl.ds(2 * p, 2)], s_in.at[p]) for p in range(PAIRS)
    ]
    small = [
        pltpu.make_async_copy(a, b, s_small.at[n])
        for n, (a, b) in enumerate(((diel_in, diel), (owner_in, owner), (slots_in, slots)))
    ]
    for p in ORDER:
        loads[p].start()
    for copy in small:
        copy.start()

    barrier = pltpu.get_barrier_semaphore()
    for dg in range(GROUPS):
        for dc in range(2):
            if dg or dc:
                to = (lax.rem(g + dg, GROUPS), gx, 2 * zl + (c if dc == 0 else 1 - c))
                pl.semaphore_signal(barrier, inc=1, device_id=to, device_id_type=MESH)
    across = (g, gx, lax.rem(gy + 3 + 2 * c, 4))
    for to in (left, across):
        pl.semaphore_signal(barrier, inc=1, device_id=to, device_id_type=MESH)

    def pack(p, which):
        def body(f, carry):
            for xx in range(2):
                x = 2 * p + xx
                at = pl.multiple_of(24 * f, 8)
                for wi in which:
                    o = 12 * xx
                    if wi == 0:
                        send[p, wi, f, o : o + 2, :] = yr[0, f, 2 * x : 2 * x + 2, :]
                        send[p, wi, f, o + 2 : o + 12, :] = orb[f, x, 0:10, :]
                    elif wi == 3:
                        send[p, wi, f, o : o + 10, :] = orb[f, x, 30:40, :]
                        send[p, wi, f, o + 10 : o + 12, :] = yr[1, f, 2 * x : 2 * x + 2, :]
                    else:
                        send[p, wi, f, o : o + 12, :] = orb[f, x, STARTS[wi] : STARTS[wi] + 12, :]
            return carry

        lax.fori_loop(0, RES, body, 0)

    def share_copy(p, wi):
        to = (2 * c + wi // 2, gx, 2 * zl + wi % 2)
        here = jnp.logical_and(to[0] == g, c == wi % 2)
        away = remote(send.at[p, wi], rb.at[p + 1, g], s_send.at[p, wi], r_send.at[p, g], to)
        near = pltpu.make_async_copy(send.at[p, wi], rb.at[p + 1, g], l_send.at[p])
        return here, away, near

    def share_start(p, wi):
        here, away, near = share_copy(p, wi)
        pl.when(here)(near.start)
        pl.when(jnp.logical_not(here))(away.start)

    def share_sent(p, wi):
        here, away, near = share_copy(p, wi)
        pl.when(jnp.logical_not(here))(away.wait_send)

    def share_arrived(p, source):
        near_one = jnp.logical_and(g == source, mine)
        near = pltpu.make_async_copy(send.at[p, 0], rb.at[p + 1, source], l_send.at[p])
        away = remote(send.at[p, 0], rb.at[p + 1, source], s_send.at[p, 0], r_send.at[p, source], sibling)
        pl.when(near_one)(near.wait)
        pl.when(jnp.logical_not(near_one))(away.wait_recv)

    loads[0].wait()
    pack(0, (1, 2))
    pl.semaphore_wait(barrier, 9)
    pl.semaphore_signal(ready, inc=1, device_id=right, device_id_type=MESH)
    share_start(0, 1)
    share_start(0, 2)
    for copy in loads[1:] + small:
        copy.wait()

    def pack_ends(f, carry):
        for x in range(XS):
            ys[0, f, 2 * x : 2 * x + 2, :] = orb[f, x, 0:2, :]
            ys[1, f, 2 * x : 2 * x + 2, :] = orb[f, x, 38:40, :]
        return carry

    lax.fori_loop(0, RES, pack_ends, 0)
    for x in range(XS):
        ys[0, RES, 2 * x : 2 * x + 2, :] = diel[x, 0:2, :]
        ys[1, RES, 2 * x : 2 * x + 2, :] = diel[x, 38:40, :]
    to_down = remote(ys.at[0], yr.at[1], s_y.at[0], r_y.at[1], down)
    to_up = remote(ys.at[1], yr.at[0], s_y.at[1], r_y.at[0], up)
    to_down.start()
    to_up.start()

    pack(4, (1, 2))
    share_start(4, 1)
    share_start(4, 2)
    to_down.wait()
    to_up.wait()
    for ch in range(2):
        for ph in range(2):

            @pl.when(jnp.logical_and(mine, jnp.logical_and(c == ch, part == ph)))
            def _():
                for k in range(2):
                    wi = 2 * ph + k
                    for x in range(XS):
                        p, o = x // 2, ROW * (x % 2)
                        if wi == 0:
                            ds_[k, p, o : o + 2, :] = yr[0, RES, 2 * x : 2 * x + 2, :]
                            ds_[k, p, o + 2 : o + 14, :] = diel[x, 0:12, :]
                        elif wi == 3:
                            ds_[k, p, o : o + 12, :] = diel[x, 28:40, :]
                            ds_[k, p, o + 12 : o + 14, :] = yr[1, RES, 2 * x : 2 * x + 2, :]
                        else:
                            ds_[k, p, o : o + 14, :] = diel[x, 10 * wi - 2 : 10 * wi + 12, :]
                near = pltpu.make_async_copy(ds_.at[ch], db.at[pl.ds(1, PAIRS)], l_d)
                away = remote(ds_.at[1 - ch], db.at[pl.ds(1, PAIRS)], s_d, r_d, sibling)
                near.start()
                away.start()

    for p in ORDER[:2]:
        pack(p, (0, 3))
        share_start(p, 0)
        share_start(p, 3)

    pack(1, (0, 1, 2, 3))
    share_start(1, 1)
    share_start(1, 2)
    for p in ORDER[3:]:
        pack(p, (0, 1, 2, 3))

    @pl.when(mine)
    def _():
        pltpu.make_async_copy(ds_.at[0], db.at[pl.ds(1, PAIRS)], l_d).wait()
        remote(ds_.at[0], db.at[pl.ds(1, PAIRS)], s_d, r_d, sibling).wait_send()

    @pl.when(jnp.logical_not(mine))
    def _():
        remote(ds_.at[0], db.at[pl.ds(1, PAIRS)], s_d, r_d, sibling).wait_recv()

    d_left = remote(db.at[1], db.at[6], s_dx.at[0], r_dx.at[0], left)
    d_right = remote(db.at[5], db.at[0], s_dx.at[1], r_dx.at[1], right)
    pl.semaphore_wait(ready, 1)
    d_left.start()
    d_right.start()

    def sib_copy(p):
        return remote(sib_s.at[p], sib_r.at[p + 1], s_sib.at[p], r_sib.at[p], sibling)

    def arrive(p):
        for source in range(GROUPS):
            share_arrived(p, source)
        for ch in range(2):

            @pl.when(c == ch)
            def _():
                def body(o, carry):
                    q, f = o // RES, lax.rem(o, RES)
                    for xx in range(2):
                        a = 12 * xx + (10 if ch == 0 else 0)
                        sib_s[p, o, 2 * xx : 2 * xx + 2, :] = rb[p + 1, q, f, a : a + 2, :]
                    return carry

                lax.fori_loop(0, ORBS, body, 0, unroll=4)

        sib_copy(p).start()

    def edge_copies(p):
        to, slot, n = (left, 6, 0) if p == 0 else (right, 0, 1)
        return (
            remote(rb.at[p + 1], rb.at[slot], s_x.at[n], r_x.at[n], to),
            remote(sib_r.at[p + 1], sib_r.at[slot], s_xs.at[n], r_xs.at[n], to),
        )

    def put(o, r, v, first, count):
        for ref, value in ((w, v), (wz, ahead(v)), (wz2, ahead(v, 2))):
            ref[o, r : r + count, :] = value[first : first + count]

    def unpack_main(slot):
        for ch in range(2):

            @pl.when(c == ch)
            def _():
                def body(o, carry):
                    q, f = o // RES, lax.rem(o, RES)
                    for xx in range(2):
                        r = BASE + 28 * slot + ROW * xx + 2 * ch
                        for n in (0, 4):
                            put(o, r + n, rb[slot, q, f, 12 * xx + n : 12 * xx + n + 8, :], 0, 8)
                    return carry

                lax.fori_loop(0, ORBS, body, 0, unroll=8)

    def unpack_sib(slot):
        for ch in range(2):

            @pl.when(c == ch)
            def _():
                def body(o, carry):
                    v = sib_r[slot, o, :, :]
                    for xx in range(2):
                        put(o, BASE + 28 * slot + ROW * xx + 12 * (1 - ch), v, 2 * xx, 2)
                    return carry

                lax.fori_loop(0, ORBS, body, 0, unroll=32)

    def unpack(slot):
        unpack_main(slot)
        unpack_sib(slot)

    def density(k, carry):
        r = pl.multiple_of(FIRST - LEAD + 8 * k, 8)
        d = pl.multiple_of(8 * k, 8)

        def body(i, acc):
            for n in range(4):
                o = 4 * i + n

                def row(ref, shift=0):
                    return ref[o, pl.ds(r + shift, 8), :]

                a, b, b2 = row(w), row(w, 14), row(w, 28)
                y1, y2, xy = row(w, 1), row(w, 2), row(w, 15)
                az, az2, bz, yz = row(wz), row(wz2), row(wz, 14), row(wz, 1)
                terms = (
                    a * a, a * b, a * y1, a * az, a * b2, a * y2, a * az2,
                    a * xy, b * y1, a * bz, az * b, a * yz, az * y1,
                )
                acc = tuple(s + t for s, t in zip(acc, terms))
            return acc

        acc = lax.fori_loop(0, ORBS // 4, body, (jnp.zeros((8, 128), F32),) * 13)
        for n in range(13):
            dens[n, pl.ds(d, 8), :] = coup[n, pl.ds(d, 8), :] * acc[n]
        return carry

    chosen = [owner[n // 4] * RES + slots[n // 4, n % 4] for n in range(8)]

    def apply(k, carry):
        r = pl.multiple_of(FIRST + 8 * k, 8)
        d = pl.multiple_of(LEAD + 8 * k, 8)

        def m(n, back=0):
            return dens[n, pl.ds(d - back, 8), :]

        level = (
            (0, m(0)), (14, m(1)), (-14, m(1, 14)), (1, m(2)), (-1, m(2, 1)), (28, m(4)), (-28, m(4, 28)),
            (2, m(5)), (-2, m(5, 2)), (15, m(7)), (-15, m(7, 15)), (13, m(8, 1)), (-13, m(8, 14)),
        )
        z1, z2 = m(3), m(6)
        lower = ((0, z1), (14, m(10)), (-14, m(9, 14)), (1, m(12)), (-1, m(11, 1)))
        upper = ((0, z1), (14, m(9)), (-14, m(10, 14)), (1, m(11)), (-1, m(12, 1)))
        for n in range(8):
            o = chosen[n]
            v = {s: w[o, pl.ds(r + s, 8), :] for s, _ in level}

            def total(terms):
                while len(terms) > 1:
                    terms = [sum(terms[i + 1 : i + 2], terms[i]) for i in range(0, len(terms), 2)]
                return terms[0]

            below = total([x * v[s] for s, x in lower])
            res = total(
                [x * v[s] for s, x in level]
                + [x * wz[o, pl.ds(r + s, 8), :] for s, x in upper]
                + [z2 * wz2[o, pl.ds(r, 8), :]]
            )
            res = res + pltpu.roll(below, 1, 1) + pltpu.roll(z2 * v[0], 2, 1)
            flat[n, pl.ds(pl.multiple_of(8 * k, 8), 8), :] = res
        return carry

    def out_copy(piece, j):
        to = (j, gx, 2 * zl + home)
        here = jnp.logical_and(g == j, mine)
        slot = 2 * part + c
        source, target = ob.at[piece], orr.at[piece]
        away = remote(source.at[j], target.at[slot], s_o.at[piece, j], r_o.at[piece, slot], to)
        near = pltpu.make_async_copy(source.at[j], target.at[slot], l_o.at[piece])
        return here, away, near

    def out_start(piece):
        first = PIECES[piece]

        def pack_out(j, carry):
            for window in range(2):
                for n in range(2):
                    o, x = 10 * (2 * window + n), first + n
                    ob[piece, j, o : o + 10, :] = flat[4 * window + j, ROW * x : ROW * x + 10, :]
            return carry

        lax.fori_loop(0, GROUPS, pack_out, 0)
        for j in range(GROUPS):
            here, away, near = out_copy(piece, j)
            pl.when(here)(near.start)
            pl.when(jnp.logical_not(here))(away.start)

    def out_place(piece):
        first = PIECES[piece]
        source, target = ob.at[piece], orr.at[piece]
        for wi in range(4):
            here = jnp.logical_and(2 * c + wi // 2 == g, c == wi % 2)
            away = remote(source.at[0], target.at[wi], s_o.at[piece, 0], r_o.at[piece, wi], sibling)
            near = pltpu.make_async_copy(source.at[0], target.at[wi], l_o.at[piece])
            pl.when(here)(near.wait)
            pl.when(jnp.logical_not(here))(away.wait_recv)
            for window in range(2):
                for n in range(2):
                    o = 10 * (2 * window + n)
                    out[window, 0, first + n, 10 * wi : 10 * wi + 10, :] = target[wi, o : o + 10, :]

    arrive(0)
    edge_copies(0)[0].start()
    for wi in range(4):
        share_sent(0, wi)
    share_start(1, 0)
    share_start(1, 3)
    arrive(4)
    edge_copies(4)[0].start()
    for wi in range(4):
        share_sent(4, wi)
    share_start(3, 1)
    share_start(3, 2)
    share_start(3, 0)
    share_start(3, 3)

    d_left.wait()
    d_right.wait()
    wd[...] = jnp.zeros_like(wd)
    for s in range(7):
        wd[BASE + 28 * s : BASE + 28 * s + 28, :] = db[s, 0:28, :]

    lane = lax.broadcasted_iota(jnp.int32, (8, 128), 1)
    top, bottom = lane == 127, lane == 0

    def ahead(v, n=1):
        return pltpu.roll(v, 128 - n, 1)

    def at(ref, r, n=0):
        return ref[r + n : r + n + 8, :]

    for i in range(29):
        r = 8 * i
        if r + 14 + 8 > ROWS:
            break
        e, ex, ey = at(wd, r), at(wd, r, 14), at(wd, r, 1)
        kx[r : r + 8, :] = 0.5 * (e + ex)
        ky[r : r + 8, :] = 0.5 * (e + ey)
        kz[r : r + 8, :] = jnp.where(top, 0.0, 0.5 * (e + ahead(e)))

    def squared(r):
        e = at(wd, r)
        x1, x0, y1, y0 = at(kx, r), at(kx, r, -14), at(ky, r), at(ky, r, -1)
        z1 = at(kz, r)
        z0 = pltpu.roll(z1, 1, 1)
        ends = jnp.where(jnp.logical_or(top, bottom), e, 0.0)
        total = x1 + x0 + y1 + y0 + z1 + z0 + ends
        squares = x1 * x1 + x0 * x0 + y1 * y1 + y0 * y0 + z1 * z1 + z0 * z0
        return total, squares

    for i in range(2, 27):
        r = 8 * i
        total, squares = squared(r)
        dd[0, r : r + 8, :] = total
        dd[1, r : r + 8, :] = squares

    def couplings(k):
        r = FIRST + 8 * k
        d0, sq = at(dd.at[0], r), at(dd.at[1], r)
        x1, y1, z1 = at(kx, r), at(ky, r), at(kz, r)
        dx, dy = at(dd.at[0], r, 14), at(dd.at[0], r, 1)
        xx, yx, zx = at(kx, r, 14), at(ky, r, 14), at(kz, r, 14)
        xy, yy, zy = at(kx, r, 1), at(ky, r, 1), at(kz, r, 1)
        dz, xz, yz, zz = ahead(d0), ahead(x1), ahead(y1), ahead(z1)
        values = (
            C0 + C1 * d0 + C2 * (d0 * d0 + sq),
            -x1 * (C1 + C2 * (d0 + dx)),
            -y1 * (C1 + C2 * (d0 + dy)),
            -z1 * (C1 + C2 * (d0 + dz)),
            C2 * (x1 * xx),
            C2 * (y1 * yy),
            C2 * (z1 * zz),
            C2 * (x1 * yx + y1 * xy),
            C2 * (x1 * y1 + xy * yx),
            C2 * (x1 * zx + z1 * xz),
            C2 * (x1 * z1 + xz * zx),
            C2 * (y1 * zy + z1 * yz),
            C2 * (y1 * z1 + yz * zy),
        )
        for n, v in enumerate(values):
            coup[n, LEAD + 8 * k : LEAD + 8 * k + 8, :] = v

    for k in range(-LEAD_CHUNKS, CHUNKS):
        couplings(k)

    for p in (0, 4):
        sib_copy(p).wait()
        edge_copies(p)[1].start()
        unpack(p + 1)
    arrive(1)
    for wi in range(4):
        share_sent(1, wi)
    share_start(2, 1)
    share_start(2, 2)
    unpack_main(2)
    sib_copy(1).wait()
    unpack_sib(2)
    share_sent(3, 1)
    share_sent(3, 2)
    share_start(2, 0)
    share_start(2, 3)
    arrive(3)
    unpack_main(4)
    sib_copy(3).wait()
    unpack_sib(4)
    for p in (0, 4):
        for e in edge_copies(p):
            e.wait()
    unpack(0)
    unpack(6)
    lax.fori_loop(0, 7, density, 0)
    lax.fori_loop(0, 3, apply, 0)
    lax.fori_loop(14, 21, density, 0)
    lax.fori_loop(14, 17, apply, 0)
    share_sent(3, 0)
    share_sent(3, 3)
    share_sent(2, 1)
    share_sent(2, 2)
    share_sent(2, 0)
    share_sent(2, 3)
    out_start(0)
    out_start(1)
    arrive(2)
    unpack_main(3)
    sib_copy(2).wait()
    unpack_sib(3)
    lax.fori_loop(7, 11, density, 0)
    lax.fori_loop(3, 7, apply, 0)
    out_start(2)
    lax.fori_loop(11, 14, density, 0)
    lax.fori_loop(7, 10, apply, 0)
    out_start(3)
    lax.fori_loop(14, 15, density, 0)
    lax.fori_loop(10, 14, apply, 0)
    out_start(4)
    for piece in range(len(PIECES)):
        out_place(piece)

    for piece in range(len(PIECES)):
        for j in range(GROUPS):
            here, away, near = out_copy(piece, j)
            pl.when(jnp.logical_not(here))(away.wait_send)


def shards(orbitals, dielectric, owner_group, block_slots):
    dma = pltpu.SemaphoreType.DMA
    vmem = pl.BlockSpec(memory_space=pltpu.VMEM)

    def buf(*shape):
        return pltpu.VMEM(shape + (128,), F32)

    return pl.pallas_call(
        kernel,
        out_shape=pltpu.VMEM((2, 1, 10, 40, 128), F32),
        in_specs=[pl.BlockSpec(memory_space=pl.ANY)] * 4,
        out_specs=vmem,
        scratch_shapes=[
            buf(RES, XS, 40), buf(XS, 40), pltpu.SMEM((2,), jnp.int32), pltpu.SMEM((2, 4), jnp.int32),
            dma((PAIRS,)), dma((3,)),
            buf(PAIRS, 4, RES, 24), buf(7, GROUPS, RES, 24), buf(PAIRS, ORBS, 8), buf(7, ORBS, 8),
            buf(2, RES + 1, 24), buf(2, RES + 1, 24), buf(2, PAIRS, 32), buf(7, 32),
            buf(ORBS, ROWS), buf(ORBS, ROWS), buf(ORBS, ROWS),
            buf(ROWS), buf(ROWS), buf(ROWS), buf(ROWS), buf(2, ROWS),
            buf(13, COUP), buf(13, COUP), buf(8, CHUNKS * 8),
            buf(5, GROUPS, 40), buf(5, 4, 40),
            dma((PAIRS, 4)), dma((PAIRS, 4)), dma((PAIRS,)),
            dma((PAIRS,)), dma((PAIRS,)), dma((2,)), dma((2,)), dma((2,)), dma((2,)), dma((2,)), dma((2,)),
            dma, dma, dma, dma((2,)), dma((2,)), dma((5, GROUPS)), dma((5, 4)), dma((5,)), pltpu.SemaphoreType.REGULAR,
        ],
        compiler_params=pltpu.CompilerParams(collective_id=0, has_side_effects=True, vmem_limit_bytes=60 << 20),
        cost_estimate=pl.CostEstimate(flops=60_000_000, bytes_accessed=2_500_000, transcendentals=0),
    )(orbitals, dielectric, owner_group, block_slots)


def solution(mesh):
    in_specs = (P("orb", "gx", "gy", None), P("gx", "gy", None), P(), P())
    out_specs = P(None, "orb", "gx", "gy", None)
    return jax.shard_map(shards, mesh=mesh, in_specs=in_specs, out_specs=out_specs, check_vma=False)
```
